256 devices in a mesh: row: 16 (over z_hi, y), col: 16 (over x, z_lo, core).
Axes of the slice: x: 4, y: 4, z: 8 (z_hi: 4, z_lo: 2; z = z_hi * 2 + z_lo), core: 2. Of those that a mesh axis runs over, the one named last changes fastest.
Arguments:
- elevation: float32 [8192, 16384], P('row', 'col'), may hold values from -20 to 20
- start_controls: float32 [2048, 4096], P('row', 'col'), may hold values from -6 to 6
Outputs:
- controls: float32 [2048, 4096], P('row', 'col')
- residual: float32 [2048, 4096], P('row', 'col')
The draws below stay inside these ranges and needn't reach their ends.
All inputs are finite; a program needn't handle non-finite values.
Results may differ from the reference program's by a relative error of at most 0.0003.
Values sent between devices are 32-bit elements; how exact they have to be, the bound alone decides.
A program may use at most 64 MiB of HBM per device.

```python
import jax
import jax.numpy as jnp
from jax import lax

ITERS = 3
MROWS = 2048
MCOLS = 4096
SROWS = 8192
SCOLS = 16384


def draw_elevation(key, part):
    key = jax.random.fold_in(key, 11)
    row_pos = jnp.arange(SROWS, dtype=jnp.float32) / SROWS
    growth = jnp.exp(jnp.log(3.0) * row_pos)[:, None]
    noise = jnp.clip(jax.random.normal(key, (SROWS, SCOLS), jnp.float32), -6.0, 6.0)
    return growth * noise


def levels(rng, shape, cuts, least, top_value):
    def one(position, shards_of):
        heights = jax.random.uniform(jax.random.fold_in(jax.random.fold_in(rng, 6), position), (shards_of,), jnp.float32, least / len(cuts), top_value / len(cuts))
        return jnp.repeat(jnp.exp(heights), shape[position] // shards_of).reshape((-1,) + (1,) * (len(shape) - position - 1))

    gain = one(*cuts[0])
    for cut in cuts[1:]:
        gain = gain * one(*cut)
    return gain


def scatter_about(stream_key, dims, width, limit, shards=(), kind=jnp.bfloat16):
    values = width * jax.random.normal(stream_key, dims, jnp.float32)
    if shards:
        values = values * levels(stream_key, dims, shards, -0.22, 0.18)
    return jnp.clip(values, -limit, limit).astype(kind)


def setup_inputs(seed: int = 0) -> dict:
    keys = jax.random.split(jax.random.key(seed), 3)
    elevation = draw_elevation(jax.random.fold_in(keys[2], 71), 0)
    start_controls = scatter_about(keys[1], (MROWS, MCOLS), 1.0, 6.0, ((0, 16), (1, 16)), jnp.float32)
    return {"elevation": elevation, "start_controls": start_controls}


huber_delta = 1.5
ridge = 0.25


def cubic(fraction):
    rest = 1.0 - fraction
    cube = fraction * fraction * fraction
    square = fraction * fraction
    return (rest * rest * rest / 6.0,
            (3.0 * cube - 6.0 * square + 4.0) / 6.0,
            (-3.0 * cube + 3.0 * square + 3.0 * fraction + 1.0) / 6.0,
            cube / 6.0)


def spline_table():
    fraction = (jnp.arange(4, dtype=jnp.float32) + 0.5) / 4.0
    return jnp.stack(cubic(fraction), axis=1)


def expand_rows(field, table):
    count = field.shape[0]
    padded = jnp.pad(field, ((0, 3), (0, 0)))
    stacked = jnp.stack([padded[offset:offset + count] for offset in range(4)])
    result = jnp.einsum('pa,amx->mpx', table, stacked, precision=lax.Precision.HIGHEST)
    return result.reshape(4 * count, field.shape[1])


def expand_cols(field, table):
    count = field.shape[1]
    padded = jnp.pad(field, ((0, 0), (0, 3)))
    stacked = jnp.stack([padded[:, offset:offset + count] for offset in range(4)])
    result = jnp.einsum('qc,cxm->xmq', table, stacked, precision=lax.Precision.HIGHEST)
    return result.reshape(field.shape[0], 4 * count)


def reduce_rows(field, table):
    count = field.shape[0] // 4
    grouped = field.reshape(count, 4, field.shape[1])
    parts = jnp.einsum('pa,mpx->amx', table, grouped, precision=lax.Precision.HIGHEST)
    total = parts[0]
    for offset in range(1, 4):
        total = total + jnp.pad(parts[offset][:count - offset], ((offset, 0), (0, 0)))
    return total


def reduce_cols(field, table):
    count = field.shape[1] // 4
    grouped = field.reshape(field.shape[0], count, 4)
    parts = jnp.einsum('qc,xmq->cxm', table, grouped, precision=lax.Precision.HIGHEST)
    total = parts[0]
    for offset in range(1, 4):
        total = total + jnp.pad(parts[offset][:, :count - offset], ((0, 0), (offset, 0)))
    return total


def evaluate(field, table):
    return expand_cols(expand_rows(field, table), table)


def transposed(field, table):
    return reduce_rows(reduce_cols(field, table), table)


def reference(elevation, start_controls):
    table = spline_table()
    misfit = elevation - evaluate(start_controls, table)
    weights = huber_delta / jnp.maximum(jnp.abs(misfit), huber_delta)
    controls = start_controls
    residual = transposed(weights * misfit, table) - ridge * start_controls
    direction = residual
    norm_now = jnp.sum(residual * residual)
    for step in range(ITERS):
        image = transposed(weights * evaluate(direction, table), table) + ridge * direction
        alpha = norm_now / jnp.sum(direction * image)
        controls = controls + alpha * direction
        residual = residual - alpha * image
        norm_next = jnp.sum(residual * residual)
        direction = residual + (norm_next / norm_now) * direction
        norm_now = norm_next
    return controls, residual
```

```python
import functools

import jax
import jax.numpy as jnp
from jax import lax
from jax.experimental import pallas as pl
from jax.experimental.pallas import tpu as pltpu
from jax.sharding import PartitionSpec as P

MESH = pl.DeviceIdType.MESH
F32 = jnp.float32
BF16 = jnp.bfloat16
huber_delta = 1.5
ridge = 0.25

PAD = 16
LANES = 128


def cubic(fraction):
    rest = 1.0 - fraction
    cube = fraction * fraction * fraction
    square = fraction * fraction
    return (
        rest * rest * rest / 6.0,
        (3.0 * cube - 6.0 * square + 4.0) / 6.0,
        (-3.0 * cube + 3.0 * square + 3.0 * fraction + 1.0) / 6.0,
        cube / 6.0,
    )


TABLE = [cubic((phase + 0.5) / 4.0) for phase in range(4)]
EVEN = [TABLE[p][0] + TABLE[p][3] for p in range(2)]
ODD_OUT = [TABLE[p][0] - TABLE[p][3] for p in range(2)]
ODD_IN = [TABLE[p][1] - TABLE[p][2] for p in range(2)]


def expand4(x):
    inner = x[1] + x[2]
    lift = (x[0] + x[3]) - inner
    far = x[0] - x[3]
    near = x[1] - x[2]
    even = [inner + EVEN[p] * lift for p in range(2)]
    odd = [ODD_OUT[p] * far + ODD_IN[p] * near for p in range(2)]
    return [even[0] + odd[0], even[1] + odd[1], even[1] - odd[1], even[0] - odd[0]]


def reduce4(y):
    e0, o0 = y[0] + y[3], y[0] - y[3]
    e1, o1 = y[1] + y[2], y[1] - y[2]
    outer = EVEN[0] * e0 + EVEN[1] * e1
    inner = (e0 + e1) - outer
    far = ODD_OUT[0] * o0 + ODD_OUT[1] * o1
    near = ODD_IN[0] * o0 + ODD_IN[1] * o1
    return [outer + far, inner + near, inner - near, outer - far]


S_, R0, W0, Z0, R1, W1, Q1 = range(7)


def kernel(nr, nc, elev, start, x_out, r_out, ev, tr, sx, vec, cols, fold, wts, perm, permh, one, two,
           hs, hr, ls, s1s, s1r, s2s, s2r):
    my_r, my_c = lax.axis_index("row"), lax.axis_index("col")
    rows, width = start.shape
    span = 4 * rows
    tiles = (rows + 2 * PAD) // 8
    own_t = (PAD // 8, (PAD + rows) // 8)

    def wrap(i, n):
        return lax.rem(i + n, n)

    barrier = pltpu.get_barrier_semaphore()

    def greet(r, c):
        pl.semaphore_signal(barrier, inc=1, device_id=(r, c), device_id_type=MESH)

    near = [(dr, dc) for dr in (-1, 0, 1) for dc in (-1, 0, 1) if (dr, dc) != (0, 0)]
    for dr, dc in near:
        if dr and dc:
            greet(wrap(my_r + dr, nr), wrap(my_c + dc, nc))

    def greet_col(d, carry):
        greet(my_r, lax.rem(my_c + d, nc))
        return carry

    def greet_row(d, carry):
        greet(lax.rem(my_r + d, nr), my_c)
        return carry

    lax.fori_loop(1, nc, greet_col, 0)
    lax.fori_loop(1, nr, greet_row, 0)

    own_rows = pl.ds(4 * PAD, span)
    own_el = pltpu.make_async_copy(elev, ev.at[own_rows, pl.ds(0, 4 * width)], ls.at[0])
    own_el.start()
    own_s = pltpu.make_async_copy(start, sx.at[pl.ds(PAD, rows), pl.ds(0, width)], ls.at[1])
    own_s.start()

    n_i = lax.broadcasted_iota(jnp.int32, (512, 128), 0)
    m_i = lax.broadcasted_iota(jnp.int32, (512, 128), 1)
    for q in range(4):
        perm[:, 128 * q:128 * (q + 1)] = jnp.where(n_i == 4 * m_i + q, 1.0, 0.0).astype(BF16)
    n_h = lax.broadcasted_iota(jnp.int32, (256, 128), 0)
    m_h = lax.broadcasted_iota(jnp.int32, (256, 128), 1)
    for q in range(4):
        hit = ((m_h < 32) & (n_h == 4 * m_h + q)) | ((m_h >= 96) & (n_h == 4 * m_h - 256 + q))
        permh[:, 128 * q:128 * (q + 1)] = jnp.where(hit, 1.0, 0.0).astype(BF16)
    zero = jnp.zeros((8, LANES), F32)
    for j in range(3):
        for q in range(4):
            cols[q, j, 8 * tiles:8 * tiles + 8, :] = zero
        for k in range(16):
            fold[k, j, 0:8, :] = zero

    pl.semaphore_wait(barrier, (nr - 1) + (nc - 1) + 4)

    up, down = 48, 40
    el_from_r = {1: (span - up, up), -1: (0, down), 0: (0, span)}
    el_to_r = {1: 4 * PAD - up, -1: 4 * PAD + span, 0: 4 * PAD}
    el_from_c = {1: (4 * width - LANES, LANES), -1: (0, LANES), 0: (0, 4 * width)}
    el_to_c = {1: 4 * width + LANES, -1: 4 * width, 0: 0}
    s_from_r = {1: (rows - PAD, PAD), -1: (0, PAD), 0: (0, rows)}
    s_to_r = {1: 0, -1: PAD + rows, 0: PAD}
    s_from_c = {1: (width - LANES, LANES), -1: (0, LANES), 0: (0, width)}
    s_to_c = {1: width + LANES, -1: width, 0: 0}
    sends = []
    for k, (dr, dc) in enumerate(near):
        for which, (src, dst, fr, tor, fc, toc) in enumerate(
            ((start, sx, s_from_r, s_to_r, s_from_c, s_to_c), (elev, ev, el_from_r, el_to_r, el_from_c, el_to_c))
        ):
            (r0, rn), (c0, cn) = fr[dr], fc[dc]
            sends.append(pltpu.make_async_remote_copy(
                src_ref=src.at[pl.ds(r0, rn), pl.ds(c0, cn)],
                dst_ref=dst.at[pl.ds(tor[dr], rn), pl.ds(toc[dc], cn)],
                send_sem=hs.at[2 * k + which], recv_sem=hr.at[2 * k + which],
                device_id=(wrap(my_r + dr, nr), wrap(my_c + dc, nc)), device_id_type=MESH))
    for copy in sends:
        copy.start()

    def gather(r0, rn, c0, cn, matrix, j):
        x = ev[pl.ds(r0, rn), pl.ds(c0, cn)]
        hi = x.astype(BF16)
        rest = x - hi.astype(F32)
        mid = rest.astype(BF16)
        low = (rest - mid.astype(F32)).astype(BF16)
        m = matrix[...]
        y = jnp.dot(hi, m, preferred_element_type=F32) + jnp.dot(mid, m, preferred_element_type=F32)
        y = y + jnp.dot(low, m, preferred_element_type=F32)
        for q in range(4):
            tr[3 * q + j, pl.ds(r0, rn), :] = y[:, 128 * q:128 * (q + 1)]

    own_el.wait()

    def gather_own(b, carry):
        r0 = pl.multiple_of(4 * PAD + 128 * b, 64)
        for j in range(2):
            gather(r0, 128, 512 * j, 512, perm, j)
        return carry

    lax.fori_loop(0, span // 128, gather_own, 0)
    own_s.wait()
    for copy in sends:
        copy.wait_recv()
    for j in range(2):
        gather(0, 4 * PAD, 512 * j, 512, perm, j)
        gather(4 * PAD + span, 64, 512 * j, 512, perm, j)

    def gather_side(b, carry):
        gather(pl.multiple_of(128 * b, 128), 128, 4 * width, 256, permh, 2)
        return carry

    lax.fori_loop(0, 5, gather_side, 0)

    lane = lax.broadcasted_iota(jnp.int32, (8, LANES), 1)
    sub = lax.broadcasted_iota(jnp.int32, (8, LANES), 0)
    has_left = jnp.where(my_c > 0, 1, 0)
    has_right = jnp.where(my_c < nc - 1, 1, 0)
    side = jnp.where(lane < 64, has_right, has_left) > 0
    side_f = jnp.where(side, 1.0, 0.0)
    cell_side = ((lane < 9) & (has_right > 0)) | ((lane >= 116) & (has_left > 0))

    def inside_rows(t):
        g = rows * my_r + 8 * t - PAD + sub
        return (g >= 0) & (g < nr * rows)

    def left_shift(u, c):
        r = [pltpu.roll(x, LANES - c, 1) for x in u]
        return [jnp.where(lane < LANES - c, r[j], r[(j + 1) % 3]) for j in range(3)]

    def right_shift(u, c):
        r = [pltpu.roll(x, c, 1) for x in u]
        return [jnp.where(lane < c, r[(j - 1) % 3], r[j]) for j in range(3)]

    def at(t, off=0):
        return pl.ds(pl.multiple_of(8 * t, 8) + off, 8)

    def spread(v, t):
        x = [v] + [left_shift(v, c) for c in range(1, 4)]
        for j in range(3):
            u = expand4([x[c][j] for c in range(4)])
            for q in range(4):
                cols[q, j, at(t), :] = u[q]

    def load(slot, t):
        return [vec[slot, j, at(t), :] for j in range(3)]

    def first(t, carry):
        keep = inside_rows(t)
        parts = [sx[at(t), 0:128], sx[at(t), 128:256], jnp.where(lane < 64, sx[at(t), 256:384], sx[at(t), 384:512])]
        ok = [keep, keep, keep & side]
        v = [jnp.where(ok[j], parts[j], 0.0) for j in range(3)]
        for j in range(3):
            vec[S_, j, at(t), :] = v[j]
        spread(v, t)
        return carry

    lax.fori_loop(0, tiles, first, 0)

    def rows_first(t, carry):
        i = 8 * t + sub
        okr = inside_rows(t) & (i >= PAD - 12) & (i < PAD + rows + 9)
        for j in range(3):
            ok = okr & cell_side if j == 2 else okr
            for q in range(4):
                z = expand4([cols[q, j, at(t, a), :] for a in range(4)])
                y = []
                for p in range(4):
                    el = tr[3 * q + j, pl.ds(pl.multiple_of(32 * t, 32) + p, 8, stride=4), :]
                    misfit = el - 0.25 * z[p]
                    w = huber_delta / jnp.maximum(jnp.abs(misfit), huber_delta)
                    wts[4 * p + q, j, at(t), :] = jnp.where(ok, w * 0.0625, 0.0)
                    y.append(jnp.where(ok, w * misfit * 0.25, 0.0))
                f = reduce4(y)
                for a in range(4):
                    fold[4 * a + q, j, at(t, 8), :] = f[a]
        return carry

    def rows_next(t, carry):
        for j in range(3):
            for q in range(4):
                z = expand4([cols[q, j, at(t, a), :] for a in range(4)])
                f = reduce4([z[p] * wts[4 * p + q, j, at(t), :] for p in range(4)])
                for a in range(4):
                    fold[4 * a + q, j, at(t, 8), :] = f[a]
        return carry

    def collect(t):
        g = []
        for j in range(3):
            h = []
            for q in range(4):
                parts = [fold[4 * a + q, j, at(t, 8 - a), :] for a in range(4)]
                h.append((parts[0] + parts[1]) + (parts[2] + parts[3]))
            g.append(reduce4(h))
        out = [g[j][0] for j in range(3)]
        for c in range(1, 4):
            moved = right_shift([g[j][c] for j in range(3)], c)
            out = [out[j] + moved[j] for j in range(3)]
        rowm = jnp.where(inside_rows(t), 1.0, 0.0)
        return [out[0] * rowm, out[1] * rowm, out[2] * (rowm * side_f)]

    def finish(src, dst, scale, on):
        def body(t, carry):
            out, v = collect(t), load(src, t)
            new = [out[j] + scale * v[j] for j in range(3)]
            for j in range(3):
                vec[dst, j, at(t), :] = new[j]
            if on:
                spread(new, t)
            return carry
        return body

    def sum_begin(n, accs):
        for k, acc in enumerate(accs):
            one[n, my_c, k:k + 1, :] = jnp.sum(acc, axis=0, keepdims=True)
        if len(accs) < 8:
            one[n, my_c, len(accs):8, :] = jnp.zeros((8 - len(accs), LANES), F32)

        def send(d, carry):
            pltpu.make_async_remote_copy(
                src_ref=one.at[n, my_c], dst_ref=one.at[n, my_c], send_sem=s1s.at[n, d], recv_sem=s1r.at[n, my_c],
                device_id=(my_r, lax.rem(my_c + d, nc)), device_id_type=MESH).start()
            return carry
        lax.fori_loop(1, nc, send, 0)

    def arrive(buf, send_sem, recv_sem, n, me, count, target):
        def body(d, carry):
            src = lax.rem(me + d, count)
            pltpu.make_async_remote_copy(
                src_ref=buf.at[n, src], dst_ref=buf.at[n, src], send_sem=send_sem.at[n, d],
                recv_sem=recv_sem.at[n, src], device_id=target(src), device_id_type=MESH).wait_recv()
            return carry
        lax.fori_loop(1, count, body, 0)
        parts = [buf[n, k] for k in range(count)]
        while len(parts) > 1:
            parts = [parts[k] + parts[k + 1] for k in range(0, len(parts), 2)]
        return parts[0]

    def sum_middle(n):
        two[n, my_r] = arrive(one, s1s, s1r, n, my_c, nc, lambda s: (my_r, s))

        def send(d, carry):
            pltpu.make_async_remote_copy(
                src_ref=two.at[n, my_r], dst_ref=two.at[n, my_r], send_sem=s2s.at[n, d], recv_sem=s2r.at[n, my_r],
                device_id=(lax.rem(my_r + d, nr), my_c), device_id_type=MESH).start()
            return carry
        lax.fori_loop(1, nr, send, 0)

    def sum_end(n, count):
        total = arrive(two, s2s, s2r, n, my_r, nr, lambda s: (s, my_c))
        total = jnp.broadcast_to(jnp.sum(total, axis=1, keepdims=True), (8, LANES))
        return [total[k:k + 1, :] for k in range(count)]

    def drain(n):
        def body1(d, carry):
            pltpu.make_async_remote_copy(
                src_ref=one.at[n, my_c], dst_ref=one.at[n, my_c], send_sem=s1s.at[n, d], recv_sem=s1r.at[n, my_c],
                device_id=(my_r, lax.rem(my_c + d, nc)), device_id_type=MESH).wait_send()
            return carry

        def body2(d, carry):
            pltpu.make_async_remote_copy(
                src_ref=two.at[n, my_r], dst_ref=two.at[n, my_r], send_sem=s2s.at[n, d], recv_sem=s2r.at[n, my_r],
                device_id=(lax.rem(my_r + d, nr), my_c), device_id_type=MESH).wait_send()
            return carry
        lax.fori_loop(1, nc, body1, 0)
        lax.fori_loop(1, nr, body2, 0)

    def dots(products, count):
        def body(t, accs):
            for j in range(2):
                accs = tuple(a + p for a, p in zip(accs, products(j, t)))
            return accs
        return lax.fori_loop(own_t[0], own_t[1], body, (zero,) * count)

    def get(slot, j, t):
        return vec[slot, j, at(t), :]

    lax.fori_loop(0, 20, rows_first, 0)
    lax.fori_loop(0, 20, finish(S_, R0, -ridge, True), 0)
    lax.fori_loop(0, 19, rows_next, 0)
    lax.fori_loop(1, 19, finish(R0, W0, ridge, True), 0)

    def products0(j, t):
        r, w = get(R0, j, t), get(W0, j, t)
        return r * r, r * w

    sum_begin(0, dots(products0, 2))
    lax.fori_loop(1, 19, rows_next, 0)
    sum_middle(0)
    lax.fori_loop(1, 19, finish(W0, Z0, ridge, False), 0)
    rr0, r0w0 = sum_end(0, 2)
    alpha0 = rr0 / r0w0

    def step1(t, carry):
        r, w, z = load(R0, t), load(W0, t), load(Z0, t)
        r1 = [r[j] - alpha0 * w[j] for j in range(3)]
        w1 = [w[j] - alpha0 * z[j] for j in range(3)]
        for j in range(3):
            vec[R1, j, at(t), :] = r1[j]
            vec[W1, j, at(t), :] = w1[j]
        spread(w1, t)
        return carry

    lax.fori_loop(1, 19, step1, 0)

    def products1(j, t):
        r1, w1, w0 = get(R1, j, t), get(W1, j, t), get(W0, j, t)
        return r1 * r1, r1 * w1, r1 * w0

    sum_begin(1, dots(products1, 3))
    lax.fori_loop(1, 18, rows_next, 0)
    sum_middle(1)
    lax.fori_loop(2, 18, finish(W1, Q1, ridge, False), 0)
    rr1, r1w1, r1w0 = sum_end(1, 3)
    beta0 = rr1 / rr0
    d1s1 = r1w1 + beta0 * (2.0 * r1w0 + beta0 * r0w0)
    alpha1 = rr1 / d1s1

    def products2(j, t):
        r0, w0, z0 = get(R0, j, t), get(W0, j, t), get(Z0, j, t)
        r1, w1, q1 = get(R1, j, t), get(W1, j, t), get(Q1, j, t)
        d1 = r1 + beta0 * r0
        s1 = w1 + beta0 * w0
        z1 = q1 + beta0 * z0
        r2 = r1 - alpha1 * s1
        w2 = w1 - alpha1 * z1
        x1 = get(S_, j, t) + alpha0 * r0 + alpha1 * d1
        vec[R0, j, at(t), :] = d1
        vec[S_, j, at(t), :] = x1
        vec[R1, j, at(t), :] = r2
        vec[W1, j, at(t), :] = s1
        vec[Q1, j, at(t), :] = w2
        return r2 * r2, r2 * w2, r2 * s1

    sum_begin(2, dots(products2, 3))
    sum_middle(2)
    rr2, r2w2, r2s1 = sum_end(2, 3)
    beta1 = rr2 / rr1
    alpha2 = rr2 / (r2w2 + beta1 * (2.0 * r2s1 + beta1 * d1s1))

    def last(t, carry):
        out_rows = pl.ds(pl.multiple_of(8 * t, 8) - PAD, 8)
        for j in range(2):
            r2, d1, s1, w2 = get(R1, j, t), get(R0, j, t), get(W1, j, t), get(Q1, j, t)
            x_out[out_rows, 128 * j:128 * (j + 1)] = get(S_, j, t) + alpha2 * (r2 + beta1 * d1)
            r_out[out_rows, 128 * j:128 * (j + 1)] = r2 - alpha2 * (w2 + beta1 * s1)
        return carry

    lax.fori_loop(own_t[0], own_t[1], last, 0)
    for copy in sends:
        copy.wait_send()
    for n in range(3):
        drain(n)


def solution(mesh):
    nr, nc = mesh.shape["row"], mesh.shape["col"]

    def shards(elevation, start_controls):
        rows, width = start_controls.shape
        out = jax.ShapeDtypeStruct((rows, width), F32)
        tall = rows + 2 * PAD
        return pl.pallas_call(
            functools.partial(kernel, nr, nc),
            out_shape=(out, out),
            in_specs=[pl.BlockSpec(memory_space=pl.ANY)] * 2,
            out_specs=(pl.BlockSpec(memory_space=pltpu.VMEM),) * 2,
            scratch_shapes=[
                pltpu.VMEM((4 * tall, 4 * width + 2 * LANES), F32),
                pltpu.VMEM((12, 4 * tall, LANES), F32),
                pltpu.VMEM((tall, width + 2 * LANES), F32),
                pltpu.VMEM((7, 3, tall, LANES), F32),
                pltpu.VMEM((4, 3, tall + 8, LANES), F32),
                pltpu.VMEM((16, 3, tall + 8, LANES), F32),
                pltpu.VMEM((16, 3, tall, LANES), F32),
                pltpu.VMEM((512, 512), BF16),
                pltpu.VMEM((256, 512), BF16),
                pltpu.VMEM((3, nc, 8, LANES), F32),
                pltpu.VMEM((3, nr, 8, LANES), F32),
                pltpu.SemaphoreType.DMA((16,)),
                pltpu.SemaphoreType.DMA((16,)),
                pltpu.SemaphoreType.DMA((2,)),
                pltpu.SemaphoreType.DMA((3, nc)),
                pltpu.SemaphoreType.DMA((3, nc)),
                pltpu.SemaphoreType.DMA((3, nr)),
                pltpu.SemaphoreType.DMA((3, nr)),
            ],
            compiler_params=pltpu.CompilerParams(
                collective_id=0, has_side_effects=True, vmem_limit_bytes=50 * 1024 * 1024
            ),
        )(elevation, start_controls)

    return jax.shard_map(
        shards,
        mesh=mesh,
        in_specs=(P("row", "col"), P("row", "col")),
        out_specs=(P("row", "col"), P("row", "col")),
        check_vma=False,
    )
```

```python
import functools

import jax
import jax.numpy as jnp
from jax import lax
from jax.experimental import pallas as pl
from jax.experimental.pallas import tpu as pltpu
from jax.sharding import PartitionSpec as P

MESH = pl.DeviceIdType.MESH
F32 = jnp.float32
BF16 = jnp.bfloat16
huber_delta = 1.5
ridge = 0.25
ITERS = 3
SHIFT = 5.0
AMPLIFY = 400.0

PAD = 16
LANES = 128


def cubic(fraction):
    rest = 1.0 - fraction
    cube = fraction * fraction * fraction
    square = fraction * fraction
    return (
        rest * rest * rest / 6.0,
        (3.0 * cube - 6.0 * square + 4.0) / 6.0,
        (-3.0 * cube + 3.0 * square + 3.0 * fraction + 1.0) / 6.0,
        cube / 6.0,
    )


TABLE = [cubic((phase + 0.5) / 4.0) for phase in range(4)]
EVEN = [TABLE[p][0] + TABLE[p][3] for p in range(2)]
ODD_OUT = [TABLE[p][0] - TABLE[p][3] for p in range(2)]
ODD_IN = [TABLE[p][1] - TABLE[p][2] for p in range(2)]


def expand4(x):
    inner = x[1] + x[2]
    lift = (x[0] + x[3]) - inner
    far = x[0] - x[3]
    near = x[1] - x[2]
    even = [inner + EVEN[p] * lift for p in range(2)]
    odd = [ODD_OUT[p] * far + ODD_IN[p] * near for p in range(2)]
    return [even[0] + odd[0], even[1] + odd[1], even[1] - odd[1], even[0] - odd[0]]


def reduce4(y):
    e0, o0 = y[0] + y[3], y[0] - y[3]
    e1, o1 = y[1] + y[2], y[1] - y[2]
    outer = EVEN[0] * e0 + EVEN[1] * e1
    inner = (e0 + e1) - outer
    far = ODD_OUT[0] * o0 + ODD_OUT[1] * o1
    near = ODD_IN[0] * o0 + ODD_IN[1] * o1
    return [outer + far, inner + near, inner - near, outer - far]


def cg_scalars(nu):
    worst = []

    def form(p, q):
        total, size = None, None
        for i, a in enumerate(p):
            for j, b in enumerate(q):
                m, bound = nu[i + j]
                term = (a * b) * m
                big = jnp.abs(a * b) * bound
                total = term if total is None else total + term
                size = big if size is None else size + big
        worst.append(size / total)
        return total

    def operate(p):
        q = [SHIFT * a for a in p] + [p[-1]]
        for i in range(1, len(p)):
            q[i] = q[i] + p[i - 1]
        return q

    one = jnp.ones_like(nu[0][0])
    residual, direction = [one], [one]
    step = [None] * ITERS
    norm_now = nu[0][0]
    for k in range(ITERS):
        image = operate(direction)
        alpha = norm_now / form(direction, image)
        for i, d in enumerate(direction):
            step[i] = alpha * d if step[i] is None else step[i] + alpha * d
        residual = [residual[i] - alpha * image[i] if i < k + 1 else -(alpha * image[i]) for i in range(k + 2)]
        if k < ITERS - 1:
            norm_next = form(residual, residual)
            beta = norm_next / norm_now
            direction = [residual[i] + beta * direction[i] if i < k + 1 else residual[i] for i in range(k + 2)]
            norm_now = norm_next
    fine = one
    for w in worst:
        fine = jnp.where((w > 0.0) & (w < AMPLIFY), fine, 0.0)
    return step, residual, fine


def loop(low, high, step, body):
    def trip(k, carry):
        body([low + step * k + i for i in range(step)])
        return carry
    lax.fori_loop(0, (high - low) // step, trip, 0)


def kernel(nr, nc, elev, start, x_out, r_out, flag, ev, tr, sx, side, side_t, sent, got, sent_s, got_s, cols, fold, wts,
           s_v, v0, v1, v2, v3, perm, permh, permt, one, two, hs, hr, ls, s1s, s1r, s2s, s2r):
    my_r, my_c = lax.axis_index("row"), lax.axis_index("col")
    rows, width = start.shape
    span = 4 * rows
    tiles = (rows + 2 * PAD) // 8
    own_low, own_high = PAD // 8, (PAD + rows) // 8

    def wrap(i, n):
        return lax.rem(i + n, n)

    barrier = pltpu.get_barrier_semaphore()

    def greet(r, c):
        pl.semaphore_signal(barrier, inc=1, device_id=(r, c), device_id_type=MESH)

    near = [(dr, dc) for dr in (-1, 0, 1) for dc in (-1, 0, 1) if (dr, dc) != (0, 0)]
    for dr, dc in near:
        if dr and dc:
            greet(wrap(my_r + dr, nr), wrap(my_c + dc, nc))
    for d in range(1, nc):
        greet(my_r, lax.rem(my_c + d, nc))
    for d in range(1, nr):
        greet(lax.rem(my_r + d, nr), my_c)

    own_el = pltpu.make_async_copy(elev, ev.at[pl.ds(4 * PAD, span), pl.ds(0, 4 * width)], ls.at[0])
    own_el.start()
    own_s = pltpu.make_async_copy(start, sx.at[pl.ds(PAD, rows), pl.ds(0, width)], ls.at[1])
    own_s.start()

    n_i = lax.broadcasted_iota(jnp.int32, (512, 128), 0)
    m_i = lax.broadcasted_iota(jnp.int32, (512, 128), 1)
    for q in range(4):
        perm[:, 128 * q:128 * (q + 1)] = jnp.where(n_i == 4 * m_i + q, 1.0, 0.0).astype(BF16)
    n_h = lax.broadcasted_iota(jnp.int32, (256, 128), 0)
    m_h = lax.broadcasted_iota(jnp.int32, (256, 128), 1)
    for q in range(4):
        hit = ((m_h < 32) & (n_h == 4 * m_h + q)) | ((m_h >= 96) & (n_h == 4 * m_h - 256 + q))
        permh[:, 128 * q:128 * (q + 1)] = jnp.where(hit, 1.0, 0.0).astype(BF16)
    n_t = lax.broadcasted_iota(jnp.int32, (128, 128), 0)
    m_t = lax.broadcasted_iota(jnp.int32, (128, 128), 1)
    for q in range(4):
        hit = ((n_t < 48) & (n_t == 4 * m_t + q)) | ((n_t >= 48) & (n_t == 4 * m_t - 416 + q) & (n_t < 96))
        permt[:, 128 * q:128 * (q + 1)] = jnp.where(hit, 1.0, 0.0).astype(BF16)
    zero = jnp.zeros((8, LANES), F32)
    for j in range(3):
        for q in range(4):
            cols[q, j, 8 * tiles:8 * tiles + 8, :] = zero
        for k in range(16):
            fold[k, j, 0:8, :] = zero
    got_s[16:112, :] = jnp.zeros((96, rows), F32)
    got[96:128, :] = jnp.zeros((32, span), F32)

    def gather(x, matrix, j, r0, rn):
        hi = x.astype(BF16)
        rest = x - hi.astype(F32)
        mid = rest.astype(BF16)
        low = (rest - mid.astype(F32)).astype(BF16)
        m = matrix[...]
        y = jnp.dot(hi, m, preferred_element_type=F32) + jnp.dot(mid, m, preferred_element_type=F32)
        y = y + jnp.dot(low, m, preferred_element_type=F32)
        for q in range(4):
            tr[3 * q + j, pl.ds(r0, rn), :] = y[:, 128 * q:128 * (q + 1)]

    def gather_own(b, carry):
        r0 = pl.multiple_of(4 * PAD + 128 * b, 64)
        for j in range(2):
            gather(ev[pl.ds(r0, 128), pl.ds(512 * j, 512)], perm, j, r0, 128)
        return carry

    own_el.wait()
    own_s.wait()
    for b in range(span // 128):
        block = ev[4 * PAD + 128 * b:4 * PAD + 128 * (b + 1), :]
        sent[0:48, 128 * b:128 * (b + 1)] = block[:, 0:128].T[0:48]
        sent[48:96, 128 * b:128 * (b + 1)] = block[:, 4 * width - 128:4 * width].T[80:128]
    sent_s[0:16, :] = sx[PAD:PAD + rows, 0:128].T[0:16]
    sent_s[16:32, :] = sx[PAD:PAD + rows, width - 128:width].T[112:128]
    lax.fori_loop(0, span // 128, gather_own, 0)

    pl.semaphore_wait(barrier, (nr - 1) + (nc - 1) + 4)

    up, down = 48, 40
    el_from_r = {1: (span - up, up), -1: (0, down)}
    el_to_r = {1: 4 * PAD - up, -1: 4 * PAD + span}
    el_from_c = {1: (4 * width - LANES, LANES), -1: (0, LANES), 0: (0, 4 * width)}
    el_to_c = {1: 4 * width + LANES, -1: 4 * width, 0: 0}
    s_from_r = {1: (rows - PAD, PAD), -1: (0, PAD)}
    s_to_r = {1: 0, -1: PAD + rows}
    s_from_c = {1: (width - LANES, LANES), -1: (0, LANES), 0: (0, width)}
    s_to_c = {1: width + LANES, -1: width, 0: 0}
    sends = []

    def send_to(dr, dc, src, dst):
        k = len(sends)
        sends.append(pltpu.make_async_remote_copy(
            src_ref=src, dst_ref=dst, send_sem=hs.at[k], recv_sem=hr.at[k],
            device_id=(wrap(my_r + dr, nr), wrap(my_c + dc, nc)), device_id_type=MESH))
        sends[-1].start()

    for dr, dc in sorted(near, key=lambda o: (o[0] == 0, o[1] != 0)):
        if dr:
            for src, dst, fr, tor, fc, toc in ((elev, ev, el_from_r, el_to_r, el_from_c, el_to_c),
                                               (start, sx, s_from_r, s_to_r, s_from_c, s_to_c)):
                (r0, rn), (c0, cn) = fr[dr], fc[dc]
                send_to(dr, dc, src.at[pl.ds(r0, rn), pl.ds(c0, cn)], dst.at[pl.ds(tor[dr], rn), pl.ds(toc[dc], cn)])
        else:
            part, to_s = (pl.ds(0, 48), pl.ds(0, 16)) if dc < 0 else (pl.ds(48, 48), pl.ds(112, 16))
            send_to(dr, dc, sent.at[part], got.at[part])
            send_to(dr, dc, sent_s.at[pl.ds(0, 16) if dc < 0 else pl.ds(16, 16)], got_s.at[to_s])

    for copy in sends:
        copy.wait_recv()
    for r0 in (0, 4 * PAD + span):
        for j in range(2):
            gather(ev[r0:r0 + 64, 512 * j:512 * (j + 1)], perm, j, r0, 64)
        gather(ev[r0:r0 + 64, 4 * width:4 * width + 256], permh, 2, r0, 64)
    for b in range(span // 128):
        gather(got[:, 128 * b:128 * (b + 1)].T, permt, 2, 4 * PAD + 128 * b, 128)

    lane = lax.broadcasted_iota(jnp.int32, (8, LANES), 1)
    sub = lax.broadcasted_iota(jnp.int32, (8, LANES), 0)
    has_left = jnp.where(my_c > 0, 1, 0)
    has_right = jnp.where(my_c < nc - 1, 1, 0)
    beside = jnp.where(lane < 64, has_right, has_left) > 0
    beside_f = jnp.where(beside, 1.0, 0.0)
    cell_side = ((lane < 9) & (has_right > 0)) | ((lane >= 116) & (has_left > 0))

    side[PAD:PAD + rows, :] = got_s[...].T
    lane2 = lax.broadcasted_iota(jnp.int32, (PAD, LANES), 1)
    for r0 in (0, PAD + rows):
        side[r0:r0 + PAD, :] = jnp.where(
            lane2 < 64, sx[r0:r0 + PAD, width:width + LANES], sx[r0:r0 + PAD, width + LANES:width + 2 * LANES])

    def inside_rows(t):
        g = rows * my_r + 8 * t - PAD + sub
        return (g >= 0) & (g < nr * rows)

    def left_shift(u, c):
        r = [pltpu.roll(x, LANES - c, 1) for x in u]
        return [jnp.where(lane < LANES - c, r[j], r[(j + 1) % 3]) for j in range(3)]

    def right_shift(u, c):
        r = [pltpu.roll(x, c, 1) for x in u]
        return [jnp.where(lane < c, r[(j - 1) % 3], r[j]) for j in range(3)]

    def at(t, off=0):
        return pl.ds(pl.multiple_of(8 * t, 8) + off, 8)

    def spread(v):
        x = [v] + [left_shift(v, c) for c in range(1, 4)]
        return [expand4([x[c][j] for c in range(4)]) for j in range(3)]

    def keep_spread(u, t):
        for j in range(3):
            for q in range(4):
                cols[q, j, at(t), :] = u[j][q]

    def first(ts):
        done = []
        for t in ts:
            keep = inside_rows(t)
            parts = [sx[at(t), 0:128], sx[at(t), 128:256], side[at(t), :]]
            ok = [keep, keep, keep & beside]
            v = [jnp.where(ok[j], parts[j], 0.0) for j in range(3)]
            done.append((t, v, spread(v)))
        for t, v, u in done:
            for j in range(3):
                s_v[j, at(t), :] = v[j]
            keep_spread(u, t)

    def rows_first(ts):
        for t in ts:
            i = 8 * t + sub
            okr = inside_rows(t) & (i >= PAD - 12) & (i < PAD + rows + 9)
            for j in range(3):
                ok = okr & cell_side if j == 2 else okr
                for q in range(4):
                    z = expand4([cols[q, j, at(t, a), :] for a in range(4)])
                    y = []
                    for p in range(4):
                        el = tr[3 * q + j, pl.ds(pl.multiple_of(32 * t, 32) + p, 8, stride=4), :]
                        misfit = el - 0.25 * z[p]
                        w = huber_delta / jnp.maximum(jnp.abs(misfit), huber_delta)
                        wts[4 * p + q, j, at(t), :] = jnp.where(ok, w * 0.0625, 0.0)
                        y.append(jnp.where(ok, w * misfit * 0.25, 0.0))
                    f = reduce4(y)
                    for a in range(4):
                        fold[4 * a + q, j, at(t, 8), :] = f[a]

    def rows_next(ts):
        for t in ts:
            for j in range(3):
                for q in range(4):
                    z = expand4([cols[q, j, at(t, a), :] for a in range(4)])
                    f = reduce4([z[p] * wts[4 * p + q, j, at(t), :] for p in range(4)])
                    for a in range(4):
                        fold[4 * a + q, j, at(t, 8), :] = f[a]

    def collect(t):
        g = []
        for j in range(3):
            h = []
            for q in range(4):
                parts = [fold[4 * a + q, j, at(t, 8 - a), :] for a in range(4)]
                h.append((parts[0] + parts[1]) + (parts[2] + parts[3]))
            g.append(reduce4(h))
        out = [g[j][0] for j in range(3)]
        for c in range(1, 4):
            moved = right_shift([g[j][c] for j in range(3)], c)
            out = [out[j] + moved[j] for j in range(3)]
        rowm = jnp.where(inside_rows(t), 1.0, 0.0)
        return [out[0] * rowm, out[1] * rowm, out[2] * (rowm * beside_f)]

    def finish(src, dst, scale, on):
        def body(ts):
            done = []
            for t in ts:
                out = collect(t)
                new = [out[j] + scale * src[j, at(t), :] for j in range(3)]
                done.append((t, new, spread(new) if on else None))
            for t, new, u in done:
                for j in range(3):
                    dst[j, at(t), :] = new[j]
                if on:
                    keep_spread(u, t)
        return body

    loop(0, 20, 2, first)
    loop(0, 20, 1, rows_first)
    loop(0, 20, UF, finish(s_v, v0, -ridge, True))
    loop(0, 19, 1, rows_next)
    loop(1, 19, UF1, finish(v0, v1, ridge - SHIFT, True))
    loop(1, 19, 1, rows_next)
    loop(1, 19, UF1, finish(v1, v2, ridge - SHIFT, True))

    def moments(t, accs):
        for j in range(2):
            a, b, c = v0[j, at(t), :], v1[j, at(t), :], v2[j, at(t), :]
            energy = None
            for q in range(4):
                z = expand4([cols[q, j, at(t, k), :] for k in range(4)])
                for p in range(4):
                    e = z[p] * z[p] * wts[4 * p + q, j, at(t), :]
                    energy = e if energy is None else energy + e
            accs = tuple(x + y for x, y in zip(accs, (a * a, a * b, b * b, b * c, c * c, energy)))
        return accs

    accs = lax.fori_loop(own_low, own_high, moments, (zero,) * 6)

    for k, acc in enumerate(accs):
        one[my_c, k:k + 1, :] = jnp.sum(acc, axis=0, keepdims=True)
    one[my_c, 6:8, :] = jnp.zeros((2, LANES), F32)

    def exchange(buf, send_sem, recv_sem, me, count, target):
        copies = []
        for d in range(1, count):
            copies.append(pltpu.make_async_remote_copy(
                src_ref=buf.at[me], dst_ref=buf.at[me], send_sem=send_sem.at[d], recv_sem=recv_sem.at[me],
                device_id=target(lax.rem(me + d, count)), device_id_type=MESH))
            copies[-1].start()
        return copies

    def arrive(buf, send_sem, recv_sem, me, count, target):
        for d in range(1, count):
            src = lax.rem(me + d, count)
            pltpu.make_async_remote_copy(
                src_ref=buf.at[src], dst_ref=buf.at[src], send_sem=send_sem.at[d], recv_sem=recv_sem.at[src],
                device_id=target(src), device_id_type=MESH).wait_recv()
        parts = [buf[k] for k in range(count)]
        while len(parts) > 1:
            parts = [parts[k] + parts[k + 1] for k in range(0, len(parts), 2)]
        return parts[0]

    sends += exchange(one, s1s, s1r, my_c, nc, lambda s: (my_r, s))
    loop(1, 18, 1, rows_next)
    two[my_r] = arrive(one, s1s, s1r, my_c, nc, lambda s: (my_r, s))
    sends += exchange(two, s2s, s2r, my_r, nr, lambda s: (s, my_c))
    loop(2, 18, UF2, finish(v2, v3, ridge - SHIFT, False))
    total = arrive(two, s2s, s2r, my_r, nr, lambda s: (s, my_c))
    total = jnp.broadcast_to(jnp.sum(total, axis=1, keepdims=True), (8, LANES))
    nu = [total[k:k + 1, :] for k in range(6)]
    pairs = [(m, jnp.abs(m)) for m in nu]
    pairs[5] = (nu[5] + (ridge - SHIFT) * nu[4], nu[5] + SHIFT * nu[4])
    step, last, fine = cg_scalars(pairs)

    step, last = ([jnp.broadcast_to(k, (8, LANES)) for k in ks] for ks in (step, last))
    flag[...] = jnp.broadcast_to(fine, (8, LANES))

    def final(ts):
        for t in ts:
            out_rows = pl.ds(pl.multiple_of(8 * t, 8) - PAD, 8)
            for j in range(2):
                v = [ref[j, at(t), :] for ref in (v0, v1, v2, v3)]
                x_out[out_rows, 128 * j:128 * (j + 1)] = (
                    s_v[j, at(t), :] + ((step[0] * v[0] + step[1] * v[1]) + step[2] * v[2]))
                r_out[out_rows, 128 * j:128 * (j + 1)] = (
                    (last[0] * v[0] + last[1] * v[1]) + (last[2] * v[2] + last[3] * v[3]))

    loop(own_low, own_high, 2, final)
    for copy in sends:
        copy.wait_send()


UF, UF1, UF2 = 4, 3, 4

def from_behind(block, axis, distance):
    devices = range(lax.axis_size(axis))
    route = [(i - distance, i) for i in devices if i - distance in devices]
    return lax.ppermute(block, axis, route)


def expand_rows(field, table):
    count = field.shape[0] - 3
    outputs = []
    for phase in range(4):
        total = table[phase][0] * field[0:count]
        for offset in range(1, 4):
            total = total + table[phase][offset] * field[offset : offset + count]
        outputs.append(total)
    return jnp.stack(outputs, axis=1).reshape(4 * count, field.shape[1])


def expand_cols(field, table):
    count = field.shape[1] - 3
    outputs = []
    for phase in range(4):
        total = table[phase][0] * field[:, 0:count]
        for offset in range(1, 4):
            total = total + table[phase][offset] * field[:, offset : offset + count]
        outputs.append(total)
    return jnp.stack(outputs, axis=2).reshape(field.shape[0], 4 * count)


def reduce_rows(field, table):
    count = field.shape[0] // 4
    grouped = field.reshape(count, 4, field.shape[1])
    total = None
    for offset in range(4):
        part = table[0][offset] * grouped[:, 0]
        for phase in range(1, 4):
            part = part + table[phase][offset] * grouped[:, phase]
        placed = jnp.pad(part, ((offset, 3 - offset), (0, 0)))
        total = placed if total is None else total + placed
    return total


def reduce_cols(field, table):
    count = field.shape[1] // 4
    grouped = field.reshape(field.shape[0], count, 4)
    total = None
    for offset in range(4):
        part = table[0][offset] * grouped[:, :, 0]
        for phase in range(1, 4):
            part = part + table[phase][offset] * grouped[:, :, phase]
        placed = jnp.pad(part, ((0, 0), (offset, 3 - offset)))
        total = placed if total is None else total + placed
    return total


def extend(tile):
    below = from_behind(tile[:3], "row", -1)
    taller = jnp.concatenate([tile, below], 0)
    beside = from_behind(taller[:, :3], "col", -1)
    return jnp.concatenate([taller, beside], 1)


def fold(partial_value):
    tile_rows = partial_value.shape[0] - 3
    tile_cols = partial_value.shape[1] - 3
    beside = from_behind(partial_value[:, tile_cols:], "col", 1)
    narrow = jnp.concatenate([partial_value[:, :3] + beside, partial_value[:, 3:tile_cols]], 1)
    below = from_behind(narrow[tile_rows:], "row", 1)
    return jnp.concatenate([narrow[:3] + below, narrow[3:tile_rows]], 0)


def squares(residual):
    return lax.psum(jnp.sum(residual * residual), ("row", "col"))


def step_by_step(elevation, start_controls):
    table = TABLE

    def evaluate(tile):
        return expand_cols(expand_rows(extend(tile), table), table)

    def transposed(field):
        return fold(reduce_rows(reduce_cols(field, table), table))

    misfit = elevation - evaluate(start_controls)
    weights = huber_delta / jnp.maximum(jnp.abs(misfit), huber_delta)
    first_term = transposed(weights * misfit)
    controls = start_controls
    residual = first_term - ridge * start_controls
    direction = residual
    norm_now = squares(residual)
    for step in range(ITERS):
        image = transposed(weights * evaluate(direction)) + ridge * direction
        alpha = norm_now / lax.psum(jnp.sum(direction * image), ("row", "col"))
        controls = controls + alpha * direction
        residual = residual - alpha * image
        norm_next = squares(residual)
        direction = residual + norm_next / norm_now * direction
        norm_now = norm_next
    return (controls, residual)


def solution(mesh):
    nr, nc = mesh.shape["row"], mesh.shape["col"]

    def shards(elevation, start_controls):
        rows, width = start_controls.shape
        out = jax.ShapeDtypeStruct((rows, width), F32)
        tall = rows + 2 * PAD
        field = pltpu.VMEM((3, tall, LANES), F32)
        x, r, fine = pl.pallas_call(
            functools.partial(kernel, nr, nc),
            out_shape=(out, out, jax.ShapeDtypeStruct((8, LANES), F32)),
            in_specs=[pl.BlockSpec(memory_space=pltpu.HBM)] * 2,
            out_specs=(pl.BlockSpec(memory_space=pltpu.VMEM),) * 3,
            scratch_shapes=[
                pltpu.VMEM((4 * tall, 4 * width + 2 * LANES), F32),
                pltpu.VMEM((12, 4 * tall, LANES), F32),
                pltpu.VMEM((tall, width + 2 * LANES), F32),
                pltpu.VMEM((tall, LANES), F32),
                pltpu.VMEM((8, LANES), F32),
                pltpu.VMEM((96, 4 * rows), F32),
                pltpu.VMEM((128, 4 * rows), F32),
                pltpu.VMEM((32, rows), F32),
                pltpu.VMEM((LANES, rows), F32),
                pltpu.VMEM((4, 3, tall + 8, LANES), F32),
                pltpu.VMEM((16, 3, tall + 8, LANES), F32),
                pltpu.VMEM((16, 3, tall, LANES), F32),
                field, field, field, field, field,
                pltpu.VMEM((512, 512), BF16),
                pltpu.VMEM((256, 512), BF16),
                pltpu.VMEM((128, 512), BF16),
                pltpu.VMEM((nc, 8, LANES), F32),
                pltpu.VMEM((nr, 8, LANES), F32),
                pltpu.SemaphoreType.DMA((16,)),
                pltpu.SemaphoreType.DMA((16,)),
                pltpu.SemaphoreType.DMA((2,)),
                pltpu.SemaphoreType.DMA((nc,)),
                pltpu.SemaphoreType.DMA((nc,)),
                pltpu.SemaphoreType.DMA((nr,)),
                pltpu.SemaphoreType.DMA((nr,)),
            ],
            compiler_params=pltpu.CompilerParams(
                collective_id=0, has_side_effects=True, vmem_limit_bytes=50 * 1024 * 1024
            ),
        )(elevation, start_controls)
        return lax.cond(fine[0, 0] > 0.5, lambda: (x, r), lambda: step_by_step(elevation, start_controls))

    return jax.shard_map(
        shards,
        mesh=mesh,
        in_specs=(P("row", "col"), P("row", "col")),
        out_specs=(P("row", "col"), P("row", "col")),
        check_vma=False,
    )
```

```python
import functools

import jax
import jax.numpy as jnp
from jax import lax
from jax.experimental import pallas as pl
from jax.experimental.pallas import tpu as pltpu
from jax.sharding import PartitionSpec as P

MESH = pl.DeviceIdType.MESH
F32 = jnp.float32
BF16 = jnp.bfloat16
huber_delta = 1.5
ridge = 0.25
ITERS = 3
SHIFT = 5.0
AMPLIFY = 400.0

PAD = 16
LANES = 128


def cubic(fraction):
    rest = 1.0 - fraction
    cube = fraction * fraction * fraction
    square = fraction * fraction
    return (
        rest * rest * rest / 6.0,
        (3.0 * cube - 6.0 * square + 4.0) / 6.0,
        (-3.0 * cube + 3.0 * square + 3.0 * fraction + 1.0) / 6.0,
        cube / 6.0,
    )


TABLE = [cubic((phase + 0.5) / 4.0) for phase in range(4)]
EVEN = [TABLE[p][0] + TABLE[p][3] for p in range(2)]
ODD_OUT = [TABLE[p][0] - TABLE[p][3] for p in range(2)]
ODD_IN = [TABLE[p][1] - TABLE[p][2] for p in range(2)]


def expand4(x):
    inner = x[1] + x[2]
    lift = (x[0] + x[3]) - inner
    far = x[0] - x[3]
    near = x[1] - x[2]
    even = [inner + EVEN[p] * lift for p in range(2)]
    odd = [ODD_OUT[p] * far + ODD_IN[p] * near for p in range(2)]
    return [even[0] + odd[0], even[1] + odd[1], even[1] - odd[1], even[0] - odd[0]]


def reduce4(y):
    e0, o0 = y[0] + y[3], y[0] - y[3]
    e1, o1 = y[1] + y[2], y[1] - y[2]
    outer = EVEN[0] * e0 + EVEN[1] * e1
    inner = (e0 + e1) - outer
    far = ODD_OUT[0] * o0 + ODD_OUT[1] * o1
    near = ODD_IN[0] * o0 + ODD_IN[1] * o1
    return [outer + far, inner + near, inner - near, outer - far]


def cg_scalars(nu):
    worst = []

    def form(p, q):
        total, size = None, None
        for i, a in enumerate(p):
            for j, b in enumerate(q):
                m, bound = nu[i + j]
                term = (a * b) * m
                big = jnp.abs(a * b) * bound
                total = term if total is None else total + term
                size = big if size is None else size + big
        worst.append(size / total)
        return total

    def operate(p):
        q = [SHIFT * a for a in p] + [p[-1]]
        for i in range(1, len(p)):
            q[i] = q[i] + p[i - 1]
        return q

    one = jnp.ones_like(nu[0][0])
    residual, direction = [one], [one]
    step = [None] * ITERS
    norm_now = nu[0][0]
    for k in range(ITERS):
        image = operate(direction)
        alpha = norm_now / form(direction, image)
        for i, d in enumerate(direction):
            step[i] = alpha * d if step[i] is None else step[i] + alpha * d
        residual = [residual[i] - alpha * image[i] if i < k + 1 else -(alpha * image[i]) for i in range(k + 2)]
        if k < ITERS - 1:
            norm_next = form(residual, residual)
            beta = norm_next / norm_now
            direction = [residual[i] + beta * direction[i] if i < k + 1 else residual[i] for i in range(k + 2)]
            norm_now = norm_next
    fine = one
    for w in worst:
        fine = jnp.where((w > 0.0) & (w < AMPLIFY), fine, 0.0)
    return step, residual, fine


def loop(low, high, step, body):
    def trip(k, carry):
        body([low + step * k + i for i in range(step)])
        return carry
    full = (high - low) // step
    lax.fori_loop(0, full, trip, 0)
    if full * step < high - low:
        body([jnp.int32(t) for t in range(low + full * step, high)])


def edges(top, bottom, step, body):
    count = top[1] - top[0]

    def tile(k):
        return jnp.where(k < count, top[0] + k, bottom[0] - count + k)

    def trip(k, carry):
        body([tile(step * k + i) for i in range(step)])
        return carry
    lax.fori_loop(0, (count + bottom[1] - bottom[0]) // step, trip, 0)


def kernel(nr, nc, elev, start, xa_out, xb_out, ra_out, rb_out, flag, ev, tr, sx, side, sent_c, got_c, sent, got, sent_s, got_s, cols, fold, wts,
           s_v, v0, v1, v2, v3, perm, permt, one, two, hs, hr, ls, s1s, s1r, s2s, s2r):
    my_r, my_c = lax.axis_index("row"), lax.axis_index("col")
    rows, width = start.shape
    span = 4 * rows
    tiles = (rows + 2 * PAD) // 8
    own_low, own_high = PAD // 8, (PAD + rows) // 8

    def wrap(i, n):
        return lax.rem(i + n, n)

    barrier = pltpu.get_barrier_semaphore()

    def greet(r, c):
        pl.semaphore_signal(barrier, inc=1, device_id=(r, c), device_id_type=MESH)

    near = [(dr, dc) for dr in (-1, 0, 1) for dc in (-1, 0, 1) if (dr, dc) != (0, 0)]
    for dr, dc in near:
        if dr and dc:
            greet(wrap(my_r + dr, nr), wrap(my_c + dc, nc))
    for d in range(1, nc):
        greet(my_r, lax.rem(my_c + d, nc))
    for d in range(1, nr):
        greet(lax.rem(my_r + d, nr), my_c)

    own_el = pltpu.make_async_copy(elev, ev.at[pl.ds(4 * PAD, span), pl.ds(0, 4 * width)], ls.at[0])
    own_el.start()
    own_s = pltpu.make_async_copy(start, sx.at[pl.ds(PAD, rows), pl.ds(0, width)], ls.at[1])
    own_s.start()

    n_i = lax.broadcasted_iota(jnp.int32, (512, 128), 0)
    m_i = lax.broadcasted_iota(jnp.int32, (512, 128), 1)
    for q in range(4):
        perm[:, 128 * q:128 * (q + 1)] = jnp.where(n_i == 4 * m_i + q, 1.0, 0.0).astype(BF16)
    n_t = lax.broadcasted_iota(jnp.int32, (128, 128), 0)
    m_t = lax.broadcasted_iota(jnp.int32, (128, 128), 1)
    for q in range(4):
        hit = ((n_t < 48) & (n_t == 4 * m_t + q)) | ((n_t >= 48) & (n_t == 4 * m_t - 416 + q) & (n_t < 96))
        permt[:, 128 * q:128 * (q + 1)] = jnp.where(hit, 1.0, 0.0).astype(BF16)
    zero = jnp.zeros((8, LANES), F32)
    for j in range(3):
        for q in range(4):
            cols[q, j, 8 * tiles:8 * tiles + 8, :] = zero
        for k in range(16):
            fold[k, j, 0:8, :] = zero
    got_s[16:112, :] = jnp.zeros((96, rows), F32)
    got[96:128, :] = jnp.zeros((32, span), F32)

    def gather(x, matrix, j, r0, rn):
        hi = x.astype(BF16)
        rest = x - hi.astype(F32)
        mid = rest.astype(BF16)
        low = (rest - mid.astype(F32)).astype(BF16)
        m = matrix[...]
        y = jnp.dot(hi, m, preferred_element_type=F32) + jnp.dot(mid, m, preferred_element_type=F32)
        y = y + jnp.dot(low, m, preferred_element_type=F32)
        for k, first_row in enumerate(r0 if isinstance(r0, tuple) else (r0,)):
            for q in range(4):
                tr[4 * j + q, pl.ds(first_row, rn), :] = y[rn * k:rn * (k + 1), 128 * q:128 * (q + 1)]

    def gather_own(b, carry):
        r0 = pl.multiple_of(4 * PAD + 128 * b, 64)
        for j in range(2):
            gather(ev[pl.ds(r0, 128), pl.ds(512 * j, 512)], perm, j, r0, 128)
        return carry

    own_el.wait()
    own_s.wait()
    for b in range(span // 128):
        block = ev[4 * PAD + 128 * b:4 * PAD + 128 * (b + 1), :]
        sent[0:48, 128 * b:128 * (b + 1)] = block[:, 0:128].T[0:48]
        sent[48:96, 128 * b:128 * (b + 1)] = block[:, 4 * width - 128:4 * width].T[80:128]
    sent_s[0:16, :] = sx[PAD:PAD + rows, 0:128].T[0:16]
    sent_s[16:32, :] = sx[PAD:PAD + rows, width - 128:width].T[112:128]
    lane_c = lax.broadcasted_iota(jnp.int32, (24, LANES), 1)
    corners = [(1, 1), (1, -1), (-1, 1), (-1, -1)]
    for k, (dr, dc) in enumerate(corners):
        r0 = 4 * PAD + (span - 48 if dr > 0 else 0)
        q0 = PAD + (rows - 24 if dr > 0 else 0)
        c0, d0 = (4 * width - LANES, width - LANES) if dc > 0 else (0, 0)
        high = ev[r0:r0 + 24, c0:c0 + LANES]
        low = ev[r0 + 24:r0 + 48, c0:c0 + LANES]
        ctl = sx[q0:q0 + 24, d0:d0 + LANES]
        if dc > 0:
            high, low, ctl = pltpu.roll(high, 48, 1), pltpu.roll(low, 96, 1), pltpu.roll(ctl, 112, 1)
        else:
            low, ctl = pltpu.roll(low, 48, 1), pltpu.roll(ctl, 96, 1)
        sent_c[k] = jnp.where(lane_c < 48, high, jnp.where(lane_c < 96, low, ctl))
    lax.fori_loop(0, span // 128, gather_own, 0)

    pl.semaphore_wait(barrier, (nr - 1) + (nc - 1) + 4)

    sends = []

    def send_to(dr, dc, src, dst):
        k = len(sends)
        sends.append(pltpu.make_async_remote_copy(
            src_ref=src, dst_ref=dst, send_sem=hs.at[k], recv_sem=hr.at[k],
            device_id=(wrap(my_r + dr, nr), wrap(my_c + dc, nc)), device_id_type=MESH))
        sends[-1].start()

    for dc in (-1, 1):
        part, part_s, to_s = ((pl.ds(0, 48), pl.ds(0, 16), pl.ds(0, 16)) if dc < 0
                              else (pl.ds(48, 48), pl.ds(16, 16), pl.ds(112, 16)))
        send_to(0, dc, sent.at[part], got.at[part])
        send_to(0, dc, sent_s.at[part_s], got_s.at[to_s])
    beside_count = len(sends)
    for k, (dr, dc) in enumerate(corners):
        send_to(dr, dc, sent_c.at[k], got_c.at[k])
    up, down = 48, 40
    send_to(1, 0, start.at[pl.ds(rows - PAD, PAD)], sx.at[pl.ds(0, PAD)])
    send_to(-1, 0, start.at[pl.ds(0, PAD)], sx.at[pl.ds(PAD + rows, PAD)])
    send_to(1, 0, tr.at[pl.ds(0, 8), pl.ds(4 * PAD + span - up, up)], tr.at[pl.ds(0, 8), pl.ds(4 * PAD - up, up)])
    send_to(-1, 0, tr.at[pl.ds(0, 8), pl.ds(4 * PAD, down)], tr.at[pl.ds(0, 8), pl.ds(4 * PAD + span, down)])

    for copy in sends[:beside_count]:
        copy.wait_recv()
    for b in range(span // 128):
        gather(got[:, 128 * b:128 * (b + 1)].T, permt, 2, 4 * PAD + 128 * b, 128)

    lane = lax.broadcasted_iota(jnp.int32, (8, LANES), 1)
    sub = lax.broadcasted_iota(jnp.int32, (8, LANES), 0)
    has_left = jnp.where(my_c > 0, 1, 0)
    has_right = jnp.where(my_c < nc - 1, 1, 0)
    beside = jnp.where(lane < 64, has_right, has_left) > 0
    beside_f = jnp.where(beside, 1.0, 0.0)
    cell_side = ((lane < 9) & (has_right > 0)) | ((lane >= 116) & (has_left > 0))

    side[PAD:PAD + rows, :] = got_s[...].T

    def inside_rows(t):
        g = rows * my_r + 8 * t - PAD + sub
        return (g >= 0) & (g < nr * rows)

    def left_shift(u, c):
        r = [pltpu.roll(x, LANES - c, 1) for x in u]
        return [jnp.where(lane < LANES - c, r[j], r[(j + 1) % 3]) for j in range(3)]

    def right_shift(u, c):
        r = [pltpu.roll(x, c, 1) for x in u]
        return [jnp.where(lane < c, r[(j - 1) % 3], r[j]) for j in range(3)]

    def at(t, off=0):
        return pl.ds(pl.multiple_of(8 * t, 8) + off, 8)

    def spread(v):
        x = [v] + [left_shift(v, c) for c in range(1, 4)]
        return [expand4([x[c][j] for c in range(4)]) for j in range(3)]

    def keep_spread(u, t):
        for j in range(3):
            for q in range(4):
                cols[q, j, at(t), :] = u[j][q]

    def first(ts):
        done = []
        for t in ts:
            keep = inside_rows(t)
            parts = [sx[at(t), 0:128], sx[at(t), 128:256], side[at(t), :]]
            ok = [keep, keep, keep & beside]
            v = [jnp.where(ok[j], parts[j], 0.0) for j in range(3)]
            done.append((t, v, spread(v)))
        for t, v, u in done:
            for j in range(3):
                s_v[j, at(t), :] = v[j]
            keep_spread(u, t)

    def rows_first(ts):
        for t in ts:
            i = 8 * t + sub
            okr = inside_rows(t) & (i >= PAD - 12) & (i < PAD + rows + 9)
            for j in range(3):
                ok = okr & cell_side if j == 2 else okr
                for q in range(4):
                    z = expand4([cols[q, j, at(t, a), :] for a in range(4)])
                    y = []
                    for p in range(4):
                        el = tr[4 * j + q, pl.ds(pl.multiple_of(32 * t, 32) + p, 8, stride=4), :]
                        misfit = el - 0.25 * z[p]
                        w = huber_delta / jnp.maximum(jnp.abs(misfit), huber_delta)
                        wts[4 * p + q, j, at(t), :] = jnp.where(ok, w * 0.0625, 0.0)
                        y.append(jnp.where(ok, w * misfit * 0.25, 0.0))
                    f = reduce4(y)
                    for a in range(4):
                        fold[4 * a + q, j, at(t, 8), :] = f[a]

    def rows_next(ts):
        for t in ts:
            for j in range(3):
                for q in range(4):
                    z = expand4([cols[q, j, at(t, a), :] for a in range(4)])
                    f = reduce4([z[p] * wts[4 * p + q, j, at(t), :] for p in range(4)])
                    for a in range(4):
                        fold[4 * a + q, j, at(t, 8), :] = f[a]

    def collect(t):
        g = []
        for j in range(3):
            h = []
            for q in range(4):
                parts = [fold[4 * a + q, j, at(t, 8 - a), :] for a in range(4)]
                h.append((parts[0] + parts[1]) + (parts[2] + parts[3]))
            g.append(reduce4(h))
        out = [g[j][0] for j in range(3)]
        for c in range(1, 4):
            moved = right_shift([g[j][c] for j in range(3)], c)
            out = [out[j] + moved[j] for j in range(3)]
        rowm = jnp.where(inside_rows(t), 1.0, 0.0)
        return [out[0] * rowm, out[1] * rowm, out[2] * (rowm * beside_f)]

    def finish(src, dst, scale, on):
        def body(ts):
            done = []
            for t in ts:
                out = collect(t)
                new = [out[j] + scale * src[j, at(t), :] for j in range(3)]
                done.append((t, new, spread(new) if on else None))
            for t, new, u in done:
                for j in range(3):
                    dst[j, at(t), :] = new[j]
                if on:
                    keep_spread(u, t)
        return body

    loop(2, 18, 2, first)
    loop(2, 17, 1, rows_first)
    loop(3, 17, 4, finish(s_v, v0, -ridge, True))
    loop(3, 16, 1, rows_next)
    loop(4, 16, 4, finish(v0, v1, ridge - SHIFT, True))
    loop(4, 15, 1, rows_next)
    loop(5, 15, 5, finish(v1, v2, ridge - SHIFT, True))

    def moments(t, accs):
        for j in range(2):
            a, b, c = v0[j, at(t), :], v1[j, at(t), :], v2[j, at(t), :]
            energy = None
            for q in range(4):
                z = expand4([cols[q, j, at(t, k), :] for k in range(4)])
                for p in range(4):
                    e = z[p] * z[p] * wts[4 * p + q, j, at(t), :]
                    energy = e if energy is None else energy + e
            accs = tuple(x + y for x, y in zip(accs, (a * a, a * b, b * b, b * c, c * c, energy)))
        return accs

    accs = lax.fori_loop(5, 14, moments, (zero,) * 6)

    for copy in sends[beside_count:]:
        copy.wait_recv()
    lane2 = lax.broadcasted_iota(jnp.int32, (PAD, LANES), 1)
    lane_d = lax.broadcasted_iota(jnp.int32, (48, LANES), 1)
    turned = []
    for k, (q0, cut) in enumerate(((0, 8), (PAD + rows, 0))):
        from_left, from_right = got_c[2 * k], got_c[2 * k + 1]
        left2 = jnp.concatenate([pltpu.roll(from_left, 48, 1), from_left], 0)
        right2 = jnp.concatenate([from_right, pltpu.roll(from_right, 80, 1)], 0)
        turned.append(jnp.where(lane_d < 48, right2, left2))
        side[q0:q0 + PAD, :] = jnp.where(
            lane2 < 64, pltpu.roll(from_right[cut:cut + PAD], 32, 1), pltpu.roll(from_left[cut:cut + PAD], 16, 1))
    gather(jnp.concatenate(turned, 0), permt, 2, (4 * PAD - 48, 4 * PAD + span), 48)
    edges((0, 2), (18, 20), 4, first)
    edges((0, 2), (17, 20), 1, rows_first)
    edges((0, 3), (17, 20), 6, finish(s_v, v0, -ridge, True))
    edges((0, 3), (16, 19), 1, rows_next)
    edges((1, 4), (16, 19), 6, finish(v0, v1, ridge - SHIFT, True))
    edges((1, 4), (15, 19), 1, rows_next)
    edges((1, 5), (15, 19), 8, finish(v1, v2, ridge - SHIFT, True))
    accs = lax.fori_loop(0, 7, lambda k, a: moments(jnp.where(k < 3, 2 + k, 11 + k), a), accs)

    for k, acc in enumerate(accs):
        one[my_c, k:k + 1, :] = jnp.sum(acc, axis=0, keepdims=True)
    one[my_c, 6:8, :] = jnp.zeros((2, LANES), F32)

    def exchange(buf, send_sem, recv_sem, me, count, target):
        copies = []
        for d in range(1, count):
            copies.append(pltpu.make_async_remote_copy(
                src_ref=buf.at[me], dst_ref=buf.at[me], send_sem=send_sem.at[d], recv_sem=recv_sem.at[me],
                device_id=target(lax.rem(me + d, count)), device_id_type=MESH))
            copies[-1].start()
        return copies

    def arrive(buf, send_sem, recv_sem, me, count, target):
        for d in range(1, count):
            src = lax.rem(me + d, count)
            pltpu.make_async_remote_copy(
                src_ref=buf.at[src], dst_ref=buf.at[src], send_sem=send_sem.at[d], recv_sem=recv_sem.at[src],
                device_id=target(src), device_id_type=MESH).wait_recv()
        parts = [buf[k] for k in range(count)]
        while len(parts) > 1:
            parts = [parts[k] + parts[k + 1] for k in range(0, len(parts), 2)]
        return parts[0]

    sends += exchange(one, s1s, s1r, my_c, nc, lambda s: (my_r, s))
    loop(1, 18, 1, rows_next)
    two[my_r] = arrive(one, s1s, s1r, my_c, nc, lambda s: (my_r, s))
    sends += exchange(two, s2s, s2r, my_r, nr, lambda s: (s, my_c))
    loop(2, 18, 4, finish(v2, v3, ridge - SHIFT, False))
    total = arrive(two, s2s, s2r, my_r, nr, lambda s: (s, my_c))
    total = jnp.broadcast_to(jnp.sum(total, axis=1, keepdims=True), (8, LANES))
    nu = [total[k:k + 1, :] for k in range(6)]
    pairs = [(m, jnp.abs(m)) for m in nu]
    pairs[5] = (nu[5] + (ridge - SHIFT) * nu[4], nu[5] + SHIFT * nu[4])
    step, last, fine = cg_scalars(pairs)

    step, last = ([jnp.broadcast_to(k, (8, LANES)) for k in ks] for ks in (step, last))
    flag[0, 0] = jnp.max(fine)
    use = jnp.broadcast_to(fine, (8, LANES)) > 0.5

    def final(ts):
        for t in ts:
            out_rows = pl.ds(pl.multiple_of(8 * t, 8) - PAD, 8)
            for j in range(2):
                v = [ref[j, at(t), :] for ref in (v0, v1, v2, v3)]
                xa = (step[0] * v[0] + step[1] * v[1]) + step[2] * v[2]
                xa_out[out_rows, 128 * j:128 * (j + 1)] = jnp.where(use, xa, 0.0)
                xb_out[out_rows, 128 * j:128 * (j + 1)] = s_v[j, at(t), :]
                ra_out[out_rows, 128 * j:128 * (j + 1)] = jnp.where(use, last[0] * v[0] + last[1] * v[1], 0.0)
                rb_out[out_rows, 128 * j:128 * (j + 1)] = last[2] * v[2] + last[3] * v[3]

    loop(own_low, own_high, 2, final)
    for copy in sends:
        copy.wait_send()


def from_behind(block, axis, distance):
    devices = range(lax.axis_size(axis))
    route = [(i - distance, i) for i in devices if i - distance in devices]
    return lax.ppermute(block, axis, route)


def expand_rows(field, table):
    count = field.shape[0] - 3
    outputs = []
    for phase in range(4):
        total = table[phase][0] * field[0:count]
        for offset in range(1, 4):
            total = total + table[phase][offset] * field[offset : offset + count]
        outputs.append(total)
    return jnp.stack(outputs, axis=1).reshape(4 * count, field.shape[1])


def expand_cols(field, table):
    count = field.shape[1] - 3
    outputs = []
    for phase in range(4):
        total = table[phase][0] * field[:, 0:count]
        for offset in range(1, 4):
            total = total + table[phase][offset] * field[:, offset : offset + count]
        outputs.append(total)
    return jnp.stack(outputs, axis=2).reshape(field.shape[0], 4 * count)


def reduce_rows(field, table):
    count = field.shape[0] // 4
    grouped = field.reshape(count, 4, field.shape[1])
    total = None
    for offset in range(4):
        part = table[0][offset] * grouped[:, 0]
        for phase in range(1, 4):
            part = part + table[phase][offset] * grouped[:, phase]
        placed = jnp.pad(part, ((offset, 3 - offset), (0, 0)))
        total = placed if total is None else total + placed
    return total


def reduce_cols(field, table):
    count = field.shape[1] // 4
    grouped = field.reshape(field.shape[0], count, 4)
    total = None
    for offset in range(4):
        part = table[0][offset] * grouped[:, :, 0]
        for phase in range(1, 4):
            part = part + table[phase][offset] * grouped[:, :, phase]
        placed = jnp.pad(part, ((0, 0), (offset, 3 - offset)))
        total = placed if total is None else total + placed
    return total


def extend(tile):
    below = from_behind(tile[:3], "row", -1)
    taller = jnp.concatenate([tile, below], 0)
    beside = from_behind(taller[:, :3], "col", -1)
    return jnp.concatenate([taller, beside], 1)


def fold(partial_value):
    tile_rows = partial_value.shape[0] - 3
    tile_cols = partial_value.shape[1] - 3
    beside = from_behind(partial_value[:, tile_cols:], "col", 1)
    narrow = jnp.concatenate([partial_value[:, :3] + beside, partial_value[:, 3:tile_cols]], 1)
    below = from_behind(narrow[tile_rows:], "row", 1)
    return jnp.concatenate([narrow[:3] + below, narrow[3:tile_rows]], 0)


def squares(residual):
    return lax.psum(jnp.sum(residual * residual), ("row", "col"))


def step_by_step(elevation, start_controls):
    table = TABLE

    def evaluate(tile):
        return expand_cols(expand_rows(extend(tile), table), table)

    def transposed(field):
        return fold(reduce_rows(reduce_cols(field, table), table))

    misfit = elevation - evaluate(start_controls)
    weights = huber_delta / jnp.maximum(jnp.abs(misfit), huber_delta)
    first_term = transposed(weights * misfit)
    controls = start_controls
    residual = first_term - ridge * start_controls
    direction = residual
    norm_now = squares(residual)
    for step in range(ITERS):
        image = transposed(weights * evaluate(direction)) + ridge * direction
        alpha = norm_now / lax.psum(jnp.sum(direction * image), ("row", "col"))
        controls = controls + alpha * direction
        residual = residual - alpha * image
        norm_next = squares(residual)
        direction = residual + norm_next / norm_now * direction
        norm_now = norm_next
    return (controls, residual)


def solution(mesh):
    nr, nc = mesh.shape["row"], mesh.shape["col"]

    def shards(elevation, start_controls):
        rows, width = start_controls.shape
        out = jax.ShapeDtypeStruct((rows, width), F32)
        tall = rows + 2 * PAD
        field = pltpu.VMEM((3, tall, LANES), F32)
        xa, xb, ra, rb, fine = pl.pallas_call(
            functools.partial(kernel, nr, nc),
            out_shape=(out, out, out, out, jax.ShapeDtypeStruct((1, 1), F32)),
            in_specs=[pl.BlockSpec(memory_space=pltpu.HBM)] * 2,
            out_specs=(pl.BlockSpec(memory_space=pltpu.VMEM),) * 4 + (pl.BlockSpec(memory_space=pltpu.SMEM),),
            scratch_shapes=[
                pltpu.VMEM((4 * tall, 4 * width), F32),
                pltpu.VMEM((12, 4 * tall, LANES), F32),
                pltpu.VMEM((tall, width), F32),
                pltpu.VMEM((tall, LANES), F32),
                pltpu.VMEM((4, 24, LANES), F32),
                pltpu.VMEM((4, 24, LANES), F32),
                pltpu.VMEM((96, 4 * rows), F32),
                pltpu.VMEM((128, 4 * rows), F32),
                pltpu.VMEM((32, rows), F32),
                pltpu.VMEM((LANES, rows), F32),
                pltpu.VMEM((4, 3, tall + 8, LANES), F32),
                pltpu.VMEM((16, 3, tall + 8, LANES), F32),
                pltpu.VMEM((16, 3, tall, LANES), F32),
                field, field, field, field, field,
                pltpu.VMEM((512, 512), BF16),
                pltpu.VMEM((128, 512), BF16),
                pltpu.VMEM((nc, 8, LANES), F32),
                pltpu.VMEM((nr, 8, LANES), F32),
                pltpu.SemaphoreType.DMA((16,)),
                pltpu.SemaphoreType.DMA((16,)),
                pltpu.SemaphoreType.DMA((2,)),
                pltpu.SemaphoreType.DMA((nc,)),
                pltpu.SemaphoreType.DMA((nc,)),
                pltpu.SemaphoreType.DMA((nr,)),
                pltpu.SemaphoreType.DMA((nr,)),
            ],
            compiler_params=pltpu.CompilerParams(
                collective_id=0, has_side_effects=True, vmem_limit_bytes=60 * 1024 * 1024
            ),
        )(elevation, start_controls)
        x, r = lax.cond(fine[0, 0] > 0.5, lambda: (xb, rb), lambda: step_by_step(elevation, start_controls))
        return xa + x, ra + r

    return jax.shard_map(
        shards,
        mesh=mesh,
        in_specs=(P("row", "col"), P("row", "col")),
        out_specs=(P("row", "col"), P("row", "col")),
        check_vma=False,
    )
```

```python
import functools

import jax
import jax.numpy as jnp
from jax import lax
from jax.experimental import pallas as pl
from jax.experimental.pallas import tpu as pltpu
from jax.sharding import PartitionSpec as P

MESH = pl.DeviceIdType.MESH
F32 = jnp.float32
BF16 = jnp.bfloat16
huber_delta = 1.5
ridge = 0.25
ITERS = 3
SHIFT = 5.0
AMPLIFY = 400.0

PAD = 16
LANES = 128


def cubic(fraction):
    rest = 1.0 - fraction
    cube = fraction * fraction * fraction
    square = fraction * fraction
    return (
        rest * rest * rest / 6.0,
        (3.0 * cube - 6.0 * square + 4.0) / 6.0,
        (-3.0 * cube + 3.0 * square + 3.0 * fraction + 1.0) / 6.0,
        cube / 6.0,
    )


TABLE = [cubic((phase + 0.5) / 4.0) for phase in range(4)]
EVEN = [TABLE[p][0] + TABLE[p][3] for p in range(2)]
ODD_OUT = [TABLE[p][0] - TABLE[p][3] for p in range(2)]
ODD_IN = [TABLE[p][1] - TABLE[p][2] for p in range(2)]


def expand4(x):
    inner = x[1] + x[2]
    lift = (x[0] + x[3]) - inner
    far = x[0] - x[3]
    near = x[1] - x[2]
    even = [inner + EVEN[p] * lift for p in range(2)]
    odd = [ODD_OUT[p] * far + ODD_IN[p] * near for p in range(2)]
    return [even[0] + odd[0], even[1] + odd[1], even[1] - odd[1], even[0] - odd[0]]


def reduce4(y):
    e0, o0 = y[0] + y[3], y[0] - y[3]
    e1, o1 = y[1] + y[2], y[1] - y[2]
    outer = EVEN[0] * e0 + EVEN[1] * e1
    inner = (e0 + e1) - outer
    far = ODD_OUT[0] * o0 + ODD_OUT[1] * o1
    near = ODD_IN[0] * o0 + ODD_IN[1] * o1
    return [outer + far, inner + near, inner - near, outer - far]


def cg_scalars(nu):
    worst = []

    def form(p, q):
        total, size = None, None
        for i, a in enumerate(p):
            for j, b in enumerate(q):
                m, bound = nu[i + j]
                term = (a * b) * m
                big = jnp.abs(a * b) * bound
                total = term if total is None else total + term
                size = big if size is None else size + big
        worst.append(size / total)
        return total

    def operate(p):
        q = [SHIFT * a for a in p] + [p[-1]]
        for i in range(1, len(p)):
            q[i] = q[i] + p[i - 1]
        return q

    one = jnp.ones_like(nu[0][0])
    residual, direction = [one], [one]
    step = [None] * ITERS
    norm_now = nu[0][0]
    for k in range(ITERS):
        image = operate(direction)
        alpha = norm_now / form(direction, image)
        for i, d in enumerate(direction):
            step[i] = alpha * d if step[i] is None else step[i] + alpha * d
        residual = [residual[i] - alpha * image[i] if i < k + 1 else -(alpha * image[i]) for i in range(k + 2)]
        if k < ITERS - 1:
            norm_next = form(residual, residual)
            beta = norm_next / norm_now
            direction = [residual[i] + beta * direction[i] if i < k + 1 else residual[i] for i in range(k + 2)]
            norm_now = norm_next
    fine = one
    for w in worst:
        fine = jnp.where((w > 0.0) & (w < AMPLIFY), fine, 0.0)
    return step, residual, fine


def loop(low, high, step, body):
    def trip(k, carry):
        body([low + step * k + i for i in range(step)])
        return carry
    full = (high - low) // step
    lax.fori_loop(0, full, trip, 0)
    if full * step < high - low:
        body([jnp.int32(t) for t in range(low + full * step, high)])


def edges(top, bottom, step, body):
    count = top[1] - top[0]

    def tile(k):
        return jnp.where(k < count, top[0] + k, bottom[0] - count + k)

    def trip(k, carry):
        body([tile(step * k + i) for i in range(step)])
        return carry
    lax.fori_loop(0, (count + bottom[1] - bottom[0]) // step, trip, 0)


def kernel(nr, nc, elev, start, xa_out, xb_out, ra_out, rb_out, flag, ev, tr, sx, side, sent_c, got_c, sent, got, sent_s, got_s, cols, fold, wts,
           s_v, v0, v1, v2, v3, perm, permt, one, two, hs, hr, ls, s1s, s1r, s2s, s2r):
    my_r, my_c = lax.axis_index("row"), lax.axis_index("col")
    rows, width = start.shape
    span = 4 * rows
    tiles = (rows + 2 * PAD) // 8
    own_low, own_high = PAD // 8, (PAD + rows) // 8

    def wrap(i, n):
        return lax.rem(i + n, n)

    barrier = pltpu.get_barrier_semaphore()

    def greet(r, c):
        pl.semaphore_signal(barrier, inc=1, device_id=(r, c), device_id_type=MESH)

    near = [(dr, dc) for dr in (-1, 0, 1) for dc in (-1, 0, 1) if (dr, dc) != (0, 0)]
    for dr, dc in near:
        if dr and dc:
            greet(wrap(my_r + dr, nr), wrap(my_c + dc, nc))
    for d in range(1, nc):
        greet(my_r, lax.rem(my_c + d, nc))
    for d in range(1, nr):
        greet(lax.rem(my_r + d, nr), my_c)

    own_el = pltpu.make_async_copy(elev, ev.at[pl.ds(4 * PAD, span), pl.ds(0, 4 * width)], ls.at[0])
    own_el.start()
    own_s = pltpu.make_async_copy(start, sx.at[pl.ds(PAD, rows), pl.ds(0, width)], ls.at[1])
    own_s.start()

    n_i = lax.broadcasted_iota(jnp.int32, (512, 128), 0)
    m_i = lax.broadcasted_iota(jnp.int32, (512, 128), 1)
    for q in range(4):
        perm[:, 128 * q:128 * (q + 1)] = jnp.where(n_i == 4 * m_i + q, 1.0, 0.0).astype(BF16)
    n_t = lax.broadcasted_iota(jnp.int32, (128, 128), 0)
    m_t = lax.broadcasted_iota(jnp.int32, (128, 128), 1)
    for q in range(4):
        hit = ((n_t < 48) & (n_t == 4 * m_t + q)) | ((n_t >= 48) & (n_t == 4 * m_t - 416 + q) & (n_t < 96))
        permt[:, 128 * q:128 * (q + 1)] = jnp.where(hit, 1.0, 0.0).astype(BF16)
    zero = jnp.zeros((8, LANES), F32)
    for j in range(3):
        for q in range(4):
            cols[q, j, 8 * tiles:8 * tiles + 8, :] = zero
        for k in range(16):
            fold[k, j, 0:8, :] = zero
    got_s[16:112, :] = jnp.zeros((96, rows), F32)
    got[96:128, :] = jnp.zeros((32, span), F32)

    def gather(x, matrix, j, r0, rn):
        hi = x.astype(BF16)
        rest = x - hi.astype(F32)
        mid = rest.astype(BF16)
        low = (rest - mid.astype(F32)).astype(BF16)
        m = matrix[...]
        y = jnp.dot(hi, m, preferred_element_type=F32) + jnp.dot(mid, m, preferred_element_type=F32)
        y = y + jnp.dot(low, m, preferred_element_type=F32)
        for k, first_row in enumerate(r0 if isinstance(r0, tuple) else (r0,)):
            for q in range(4):
                tr[4 * j + q, pl.ds(first_row, rn), :] = y[rn * k:rn * (k + 1), 128 * q:128 * (q + 1)]

    def gather_own(b, carry):
        r0 = pl.multiple_of(4 * PAD + 128 * b, 64)
        for j in range(2):
            gather(ev[pl.ds(r0, 128), pl.ds(512 * j, 512)], perm, j, r0, 128)
        return carry

    own_el.wait()
    own_s.wait()
    for b in range(span // 128):
        block = ev[4 * PAD + 128 * b:4 * PAD + 128 * (b + 1), :]
        sent[0:48, 128 * b:128 * (b + 1)] = block[:, 0:128].T[0:48]
        sent[48:96, 128 * b:128 * (b + 1)] = block[:, 4 * width - 128:4 * width].T[80:128]
    sent_s[0:16, :] = sx[PAD:PAD + rows, 0:128].T[0:16]
    sent_s[16:32, :] = sx[PAD:PAD + rows, width - 128:width].T[112:128]
    lane_c = lax.broadcasted_iota(jnp.int32, (24, LANES), 1)
    corners = [(1, 1), (1, -1), (-1, 1), (-1, -1)]
    for k, (dr, dc) in enumerate(corners):
        r0 = 4 * PAD + (span - 48 if dr > 0 else 0)
        q0 = PAD + (rows - 24 if dr > 0 else 0)
        c0, d0 = (4 * width - LANES, width - LANES) if dc > 0 else (0, 0)
        high = ev[r0:r0 + 24, c0:c0 + LANES]
        low = ev[r0 + 24:r0 + 48, c0:c0 + LANES]
        ctl = sx[q0:q0 + 24, d0:d0 + LANES]
        if dc > 0:
            high, low, ctl = pltpu.roll(high, 48, 1), pltpu.roll(low, 96, 1), pltpu.roll(ctl, 112, 1)
        else:
            low, ctl = pltpu.roll(low, 48, 1), pltpu.roll(ctl, 96, 1)
        sent_c[k] = jnp.where(lane_c < 48, high, jnp.where(lane_c < 96, low, ctl))
    lax.fori_loop(0, span // 128, gather_own, 0)

    pl.semaphore_wait(barrier, (nr - 1) + (nc - 1) + 4)

    sends = []

    def send_to(dr, dc, src, dst):
        k = len(sends)
        sends.append(pltpu.make_async_remote_copy(
            src_ref=src, dst_ref=dst, send_sem=hs.at[k], recv_sem=hr.at[k],
            device_id=(wrap(my_r + dr, nr), wrap(my_c + dc, nc)), device_id_type=MESH))
        sends[-1].start()

    for dc in (-1, 1):
        part, part_s, to_s = ((pl.ds(0, 48), pl.ds(0, 16), pl.ds(0, 16)) if dc < 0
                              else (pl.ds(48, 48), pl.ds(16, 16), pl.ds(112, 16)))
        send_to(0, dc, sent.at[part], got.at[part])
        send_to(0, dc, sent_s.at[part_s], got_s.at[to_s])
    beside_count = len(sends)
    for k, (dr, dc) in enumerate(corners):
        send_to(dr, dc, sent_c.at[k], got_c.at[k])
    up, down = 48, 40
    send_to(1, 0, start.at[pl.ds(rows - PAD, PAD)], sx.at[pl.ds(0, PAD)])
    send_to(-1, 0, start.at[pl.ds(0, PAD)], sx.at[pl.ds(PAD + rows, PAD)])
    send_to(1, 0, tr.at[pl.ds(0, 8), pl.ds(4 * PAD + span - up, up)], tr.at[pl.ds(0, 8), pl.ds(4 * PAD - up, up)])
    send_to(-1, 0, tr.at[pl.ds(0, 8), pl.ds(4 * PAD, down)], tr.at[pl.ds(0, 8), pl.ds(4 * PAD + span, down)])

    for copy in sends[:beside_count]:
        copy.wait_recv()
    for b in range(span // 128):
        gather(got[:, 128 * b:128 * (b + 1)].T, permt, 2, 4 * PAD + 128 * b, 128)

    lane = lax.broadcasted_iota(jnp.int32, (8, LANES), 1)
    sub = lax.broadcasted_iota(jnp.int32, (8, LANES), 0)
    has_left = jnp.where(my_c > 0, 1, 0)
    has_right = jnp.where(my_c < nc - 1, 1, 0)
    beside = jnp.where(lane < 64, has_right, has_left) > 0
    beside_f = jnp.where(beside, 1.0, 0.0)
    cell_side = ((lane < 9) & (has_right > 0)) | ((lane >= 116) & (has_left > 0))

    side[PAD:PAD + rows, :] = got_s[...].T

    def inside_rows(t):
        g = rows * my_r + 8 * t - PAD + sub
        return (g >= 0) & (g < nr * rows)

    def left_shift(u, c):
        r = [pltpu.roll(x, LANES - c, 1) for x in u]
        return [jnp.where(lane < LANES - c, r[j], r[(j + 1) % 3]) for j in range(3)]

    def right_shift(u, c):
        r = [pltpu.roll(x, c, 1) for x in u]
        return [jnp.where(lane < c, r[(j - 1) % 3], r[j]) for j in range(3)]

    def at(t, off=0):
        return pl.ds(pl.multiple_of(8 * t, 8) + off, 8)

    def spread(v):
        x = [v] + [left_shift(v, c) for c in range(1, 4)]
        return [expand4([x[c][j] for c in range(4)]) for j in range(3)]

    def keep_spread(u, t):
        for j in range(3):
            for q in range(4):
                cols[q, j, at(t), :] = u[j][q]

    def first(ts):
        done = []
        for t in ts:
            keep = inside_rows(t)
            parts = [sx[at(t), 0:128], sx[at(t), 128:256], side[at(t), :]]
            ok = [keep, keep, keep & beside]
            v = [jnp.where(ok[j], parts[j], 0.0) for j in range(3)]
            done.append((t, v, spread(v)))
        for t, v, u in done:
            for j in range(3):
                s_v[j, at(t), :] = v[j]
            keep_spread(u, t)

    def rows_first(ts):
        for t in ts:
            i = 8 * t + sub
            okr = inside_rows(t) & (i >= PAD - 12) & (i < PAD + rows + 9)
            for j in range(3):
                ok = okr & cell_side if j == 2 else okr
                for q in range(4):
                    z = expand4([cols[q, j, at(t, a), :] for a in range(4)])
                    y = []
                    for p in range(4):
                        el = tr[4 * j + q, pl.ds(pl.multiple_of(32 * t, 32) + p, 8, stride=4), :]
                        misfit = el - 0.25 * z[p]
                        w = huber_delta / jnp.maximum(jnp.abs(misfit), huber_delta)
                        wts[4 * p + q, j, at(t), :] = jnp.where(ok, w * 0.0625, 0.0)
                        y.append(jnp.where(ok, w * misfit * 0.25, 0.0))
                    f = reduce4(y)
                    for a in range(4):
                        fold[4 * a + q, j, at(t, 8), :] = f[a]

    def rows_next(ts):
        for t in ts:
            for j in range(3):
                for q in range(4):
                    z = expand4([cols[q, j, at(t, a), :] for a in range(4)])
                    f = reduce4([z[p] * wts[4 * p + q, j, at(t), :] for p in range(4)])
                    for a in range(4):
                        fold[4 * a + q, j, at(t, 8), :] = f[a]

    def collect(t):
        g = []
        for j in range(3):
            h = []
            for q in range(4):
                parts = [fold[4 * a + q, j, at(t, 8 - a), :] for a in range(4)]
                h.append((parts[0] + parts[1]) + (parts[2] + parts[3]))
            g.append(reduce4(h))
        out = [g[j][0] for j in range(3)]
        for c in range(1, 4):
            moved = right_shift([g[j][c] for j in range(3)], c)
            out = [out[j] + moved[j] for j in range(3)]
        rowm = jnp.where(inside_rows(t), 1.0, 0.0)
        return [out[0] * rowm, out[1] * rowm, out[2] * (rowm * beside_f)]

    def finish(src, dst, scale, on):
        def body(ts):
            done = []
            for t in ts:
                out = collect(t)
                new = [out[j] + scale * src[j, at(t), :] for j in range(3)]
                done.append((t, new, spread(new) if on else None))
            for t, new, u in done:
                for j in range(3):
                    dst[j, at(t), :] = new[j]
                if on:
                    keep_spread(u, t)
        return body

    loop(2, 18, 4, first)
    loop(2, 17, 1, rows_first)
    loop(3, 17, 4, finish(s_v, v0, -ridge, True))
    loop(3, 16, 1, rows_next)
    loop(4, 16, 4, finish(v0, v1, ridge - SHIFT, True))
    loop(4, 15, 1, rows_next)
    loop(5, 15, 5, finish(v1, v2, ridge - SHIFT, True))

    def moments(t, accs):
        for j in range(2):
            a, b, c = v0[j, at(t), :], v1[j, at(t), :], v2[j, at(t), :]
            energy = None
            for q in range(4):
                z = expand4([cols[q, j, at(t, k), :] for k in range(4)])
                for p in range(4):
                    e = z[p] * z[p] * wts[4 * p + q, j, at(t), :]
                    energy = e if energy is None else energy + e
            accs = tuple(x + y for x, y in zip(accs, (a * a, a * b, b * b, b * c, c * c, energy)))
        return accs

    accs = lax.fori_loop(5, 14, moments, (zero,) * 6)

    for copy in sends[beside_count:]:
        copy.wait_recv()
    lane2 = lax.broadcasted_iota(jnp.int32, (PAD, LANES), 1)
    lane_d = lax.broadcasted_iota(jnp.int32, (48, LANES), 1)
    turned = []
    for k, (q0, cut) in enumerate(((0, 8), (PAD + rows, 0))):
        from_left, from_right = got_c[2 * k], got_c[2 * k + 1]
        left2 = jnp.concatenate([pltpu.roll(from_left, 48, 1), from_left], 0)
        right2 = jnp.concatenate([from_right, pltpu.roll(from_right, 80, 1)], 0)
        turned.append(jnp.where(lane_d < 48, right2, left2))
        side[q0:q0 + PAD, :] = jnp.where(
            lane2 < 64, pltpu.roll(from_right[cut:cut + PAD], 32, 1), pltpu.roll(from_left[cut:cut + PAD], 16, 1))
    gather(jnp.concatenate(turned, 0), permt, 2, (4 * PAD - 48, 4 * PAD + span), 48)
    edges((0, 2), (18, 20), 4, first)
    edges((0, 2), (17, 20), 1, rows_first)
    edges((0, 3), (17, 20), 6, finish(s_v, v0, -ridge, True))
    edges((0, 3), (16, 19), 1, rows_next)
    edges((1, 4), (16, 19), 6, finish(v0, v1, ridge - SHIFT, True))
    edges((1, 4), (15, 19), 1, rows_next)
    edges((1, 5), (15, 19), 8, finish(v1, v2, ridge - SHIFT, True))
    accs = lax.fori_loop(0, 7, lambda k, a: moments(jnp.where(k < 3, 2 + k, 11 + k), a), accs)

    for k, acc in enumerate(accs):
        one[my_c, k:k + 1, :] = jnp.sum(acc, axis=0, keepdims=True)
    one[my_c, 6:8, :] = jnp.zeros((2, LANES), F32)

    def exchange(buf, send_sem, recv_sem, me, count, target):
        copies = []
        for d in range(1, count):
            copies.append(pltpu.make_async_remote_copy(
                src_ref=buf.at[me], dst_ref=buf.at[me], send_sem=send_sem.at[d], recv_sem=recv_sem.at[me],
                device_id=target(lax.rem(me + d, count)), device_id_type=MESH))
            copies[-1].start()
        return copies

    def arrive(buf, send_sem, recv_sem, me, count, target):
        for d in range(1, count):
            src = lax.rem(me + d, count)
            pltpu.make_async_remote_copy(
                src_ref=buf.at[src], dst_ref=buf.at[src], send_sem=send_sem.at[d], recv_sem=recv_sem.at[src],
                device_id=target(src), device_id_type=MESH).wait_recv()
        parts = [buf[k] for k in range(count)]
        while len(parts) > 1:
            parts = [parts[k] + parts[k + 1] for k in range(0, len(parts), 2)]
        return parts[0]

    sends += exchange(one, s1s, s1r, my_c, nc, lambda s: (my_r, s))
    loop(1, 18, 1, rows_next)
    two[my_r] = arrive(one, s1s, s1r, my_c, nc, lambda s: (my_r, s))
    sends += exchange(two, s2s, s2r, my_r, nr, lambda s: (s, my_c))
    loop(2, 18, 4, finish(v2, v3, ridge - SHIFT, False))
    for copy in sends[:-(nr - 1)]:
        copy.wait_send()
    total = arrive(two, s2s, s2r, my_r, nr, lambda s: (s, my_c))
    total = jnp.broadcast_to(jnp.sum(total, axis=1, keepdims=True), (8, LANES))
    nu = [total[k:k + 1, :] for k in range(6)]
    pairs = [(m, jnp.abs(m)) for m in nu]
    pairs[5] = (nu[5] + (ridge - SHIFT) * nu[4], nu[5] + SHIFT * nu[4])
    step, last, fine = cg_scalars(pairs)

    step, last = ([jnp.broadcast_to(k, (8, LANES)) for k in ks] for ks in (step, last))
    flag[0, 0] = jnp.max(fine)
    use = jnp.broadcast_to(fine, (8, LANES)) > 0.5

    def final(ts):
        for t in ts:
            out_rows = pl.ds(pl.multiple_of(8 * t, 8) - PAD, 8)
            for j in range(2):
                v = [ref[j, at(t), :] for ref in (v0, v1, v2, v3)]
                xa = (step[0] * v[0] + step[1] * v[1]) + step[2] * v[2]
                xa_out[out_rows, 128 * j:128 * (j + 1)] = jnp.where(use, xa, 0.0)
                xb_out[out_rows, 128 * j:128 * (j + 1)] = s_v[j, at(t), :]
                ra_out[out_rows, 128 * j:128 * (j + 1)] = jnp.where(use, last[0] * v[0] + last[1] * v[1], 0.0)
                rb_out[out_rows, 128 * j:128 * (j + 1)] = last[2] * v[2] + last[3] * v[3]

    loop(own_low, own_high, 4, final)
    for copy in sends[-(nr - 1):]:
        copy.wait_send()


def from_behind(block, axis, distance):
    devices = range(lax.axis_size(axis))
    route = [(i - distance, i) for i in devices if i - distance in devices]
    return lax.ppermute(block, axis, route)


def expand_rows(field, table):
    count = field.shape[0] - 3
    outputs = []
    for phase in range(4):
        total = table[phase][0] * field[0:count]
        for offset in range(1, 4):
            total = total + table[phase][offset] * field[offset : offset + count]
        outputs.append(total)
    return jnp.stack(outputs, axis=1).reshape(4 * count, field.shape[1])


def expand_cols(field, table):
    count = field.shape[1] - 3
    outputs = []
    for phase in range(4):
        total = table[phase][0] * field[:, 0:count]
        for offset in range(1, 4):
            total = total + table[phase][offset] * field[:, offset : offset + count]
        outputs.append(total)
    return jnp.stack(outputs, axis=2).reshape(field.shape[0], 4 * count)


def reduce_rows(field, table):
    count = field.shape[0] // 4
    grouped = field.reshape(count, 4, field.shape[1])
    total = None
    for offset in range(4):
        part = table[0][offset] * grouped[:, 0]
        for phase in range(1, 4):
            part = part + table[phase][offset] * grouped[:, phase]
        placed = jnp.pad(part, ((offset, 3 - offset), (0, 0)))
        total = placed if total is None else total + placed
    return total


def reduce_cols(field, table):
    count = field.shape[1] // 4
    grouped = field.reshape(field.shape[0], count, 4)
    total = None
    for offset in range(4):
        part = table[0][offset] * grouped[:, :, 0]
        for phase in range(1, 4):
            part = part + table[phase][offset] * grouped[:, :, phase]
        placed = jnp.pad(part, ((0, 0), (offset, 3 - offset)))
        total = placed if total is None else total + placed
    return total


def extend(tile):
    below = from_behind(tile[:3], "row", -1)
    taller = jnp.concatenate([tile, below], 0)
    beside = from_behind(taller[:, :3], "col", -1)
    return jnp.concatenate([taller, beside], 1)


def fold(partial_value):
    tile_rows = partial_value.shape[0] - 3
    tile_cols = partial_value.shape[1] - 3
    beside = from_behind(partial_value[:, tile_cols:], "col", 1)
    narrow = jnp.concatenate([partial_value[:, :3] + beside, partial_value[:, 3:tile_cols]], 1)
    below = from_behind(narrow[tile_rows:], "row", 1)
    return jnp.concatenate([narrow[:3] + below, narrow[3:tile_rows]], 0)


def squares(residual):
    return lax.psum(jnp.sum(residual * residual), ("row", "col"))


def step_by_step(elevation, start_controls):
    table = TABLE

    def evaluate(tile):
        return expand_cols(expand_rows(extend(tile), table), table)

    def transposed(field):
        return fold(reduce_rows(reduce_cols(field, table), table))

    misfit = elevation - evaluate(start_controls)
    weights = huber_delta / jnp.maximum(jnp.abs(misfit), huber_delta)
    first_term = transposed(weights * misfit)
    controls = start_controls
    residual = first_term - ridge * start_controls
    direction = residual
    norm_now = squares(residual)
    for step in range(ITERS):
        image = transposed(weights * evaluate(direction)) + ridge * direction
        alpha = norm_now / lax.psum(jnp.sum(direction * image), ("row", "col"))
        controls = controls + alpha * direction
        residual = residual - alpha * image
        norm_next = squares(residual)
        direction = residual + norm_next / norm_now * direction
        norm_now = norm_next
    return (controls, residual)


def add_pairs(xa, xb, ra, rb, x, r):
    x[...] = xa[...] + xb[...]
    r[...] = ra[...] + rb[...]


def solution(mesh):
    nr, nc = mesh.shape["row"], mesh.shape["col"]

    def shards(elevation, start_controls):
        rows, width = start_controls.shape
        out = jax.ShapeDtypeStruct((rows, width), F32)
        tall = rows + 2 * PAD
        field = pltpu.VMEM((3, tall, LANES), F32)
        xa, xb, ra, rb, fine = pl.pallas_call(
            functools.partial(kernel, nr, nc),
            out_shape=(out, out, out, out, jax.ShapeDtypeStruct((1, 1), F32)),
            in_specs=[pl.BlockSpec(memory_space=pltpu.HBM)] * 2,
            out_specs=(pl.BlockSpec(memory_space=pltpu.VMEM),) * 4 + (pl.BlockSpec(memory_space=pltpu.SMEM),),
            scratch_shapes=[
                pltpu.VMEM((4 * tall, 4 * width), F32),
                pltpu.VMEM((12, 4 * tall, LANES), F32),
                pltpu.VMEM((tall, width), F32),
                pltpu.VMEM((tall, LANES), F32),
                pltpu.VMEM((4, 24, LANES), F32),
                pltpu.VMEM((4, 24, LANES), F32),
                pltpu.VMEM((96, 4 * rows), F32),
                pltpu.VMEM((128, 4 * rows), F32),
                pltpu.VMEM((32, rows), F32),
                pltpu.VMEM((LANES, rows), F32),
                pltpu.VMEM((4, 3, tall + 8, LANES), F32),
                pltpu.VMEM((16, 3, tall + 8, LANES), F32),
                pltpu.VMEM((16, 3, tall, LANES), F32),
                field, field, field, field, field,
                pltpu.VMEM((512, 512), BF16),
                pltpu.VMEM((128, 512), BF16),
                pltpu.VMEM((nc, 8, LANES), F32),
                pltpu.VMEM((nr, 8, LANES), F32),
                pltpu.SemaphoreType.DMA((16,)),
                pltpu.SemaphoreType.DMA((16,)),
                pltpu.SemaphoreType.DMA((2,)),
                pltpu.SemaphoreType.DMA((nc,)),
                pltpu.SemaphoreType.DMA((nc,)),
                pltpu.SemaphoreType.DMA((nr,)),
                pltpu.SemaphoreType.DMA((nr,)),
            ],
            compiler_params=pltpu.CompilerParams(
                collective_id=0, has_side_effects=True, vmem_limit_bytes=60 * 1024 * 1024
            ),
        )(elevation, start_controls)
        x, r = lax.cond(fine[0, 0] > 0.5, lambda: (xb, rb), lambda: step_by_step(elevation, start_controls))
        return pl.pallas_call(add_pairs, out_shape=(out, out))(xa, x, ra, r)

    return jax.shard_map(
        shards,
        mesh=mesh,
        in_specs=(P("row", "col"), P("row", "col")),
        out_specs=(P("row", "col"), P("row", "col")),
        check_vma=False,
    )
```

```python
import functools

import jax
import jax.numpy as jnp
from jax import lax
from jax.experimental import pallas as pl
from jax.experimental.pallas import tpu as pltpu
from jax.sharding import PartitionSpec as P

MESH = pl.DeviceIdType.MESH
F32 = jnp.float32
BF16 = jnp.bfloat16
huber_delta = 1.5
ridge = 0.25
ITERS = 3
SHIFT = 5.0
AMPLIFY = 400.0

PAD = 16
LANES = 128


def cubic(fraction):
    rest = 1.0 - fraction
    cube = fraction * fraction * fraction
    square = fraction * fraction
    return (
        rest * rest * rest / 6.0,
        (3.0 * cube - 6.0 * square + 4.0) / 6.0,
        (-3.0 * cube + 3.0 * square + 3.0 * fraction + 1.0) / 6.0,
        cube / 6.0,
    )


TABLE = [cubic((phase + 0.5) / 4.0) for phase in range(4)]
EVEN = [TABLE[p][0] + TABLE[p][3] for p in range(2)]
ODD_OUT = [TABLE[p][0] - TABLE[p][3] for p in range(2)]
ODD_IN = [TABLE[p][1] - TABLE[p][2] for p in range(2)]


def expand4(x):
    inner = x[1] + x[2]
    lift = (x[0] + x[3]) - inner
    far = x[0] - x[3]
    near = x[1] - x[2]
    even = [inner + EVEN[p] * lift for p in range(2)]
    odd = [ODD_OUT[p] * far + ODD_IN[p] * near for p in range(2)]
    return [even[0] + odd[0], even[1] + odd[1], even[1] - odd[1], even[0] - odd[0]]


def reduce4(y):
    e0, o0 = y[0] + y[3], y[0] - y[3]
    e1, o1 = y[1] + y[2], y[1] - y[2]
    outer = EVEN[0] * e0 + EVEN[1] * e1
    inner = (e0 + e1) - outer
    far = ODD_OUT[0] * o0 + ODD_OUT[1] * o1
    near = ODD_IN[0] * o0 + ODD_IN[1] * o1
    return [outer + far, inner + near, inner - near, outer - far]


def cg_scalars(nu):
    worst = []

    def form(p, q):
        total, size = None, None
        for i, a in enumerate(p):
            for j, b in enumerate(q):
                m, bound = nu[i + j]
                term = (a * b) * m
                big = jnp.abs(a * b) * bound
                total = term if total is None else total + term
                size = big if size is None else size + big
        worst.append(size / total)
        return total

    def operate(p):
        q = [SHIFT * a for a in p] + [p[-1]]
        for i in range(1, len(p)):
            q[i] = q[i] + p[i - 1]
        return q

    one = jnp.ones_like(nu[0][0])
    residual, direction = [one], [one]
    step = [None] * ITERS
    norm_now = nu[0][0]
    for k in range(ITERS):
        image = operate(direction)
        alpha = norm_now / form(direction, image)
        for i, d in enumerate(direction):
            step[i] = alpha * d if step[i] is None else step[i] + alpha * d
        residual = [residual[i] - alpha * image[i] if i < k + 1 else -(alpha * image[i]) for i in range(k + 2)]
        if k < ITERS - 1:
            norm_next = form(residual, residual)
            beta = norm_next / norm_now
            direction = [residual[i] + beta * direction[i] if i < k + 1 else residual[i] for i in range(k + 2)]
            norm_now = norm_next
    fine = one
    for w in worst:
        fine = jnp.where((w > 0.0) & (w < AMPLIFY), fine, 0.0)
    return step, residual, fine


def loop(low, high, step, body):
    def trip(k, carry):
        body([low + step * k + i for i in range(step)])
        return carry
    full = (high - low) // step
    lax.fori_loop(0, full, trip, 0)
    if full * step < high - low:
        body([jnp.int32(t) for t in range(low + full * step, high)])


def edges(top, bottom, step, body):
    count = top[1] - top[0]

    def tile(k):
        return jnp.where(k < count, top[0] + k, bottom[0] - count + k)

    def trip(k, carry):
        body([tile(step * k + i) for i in range(step)])
        return carry
    lax.fori_loop(0, (count + bottom[1] - bottom[0]) // step, trip, 0)


def kernel(nr, nc, elev, start, xa_out, xb_out, ra_out, rb_out, flag, ev, tr, sx, side, sent_c, got_c, sent, got, sent_s, got_s, cols, fold, wts,
           s_v, v0, v1, v2, v3, perm, permt, one, two, hs, hr, ls, s1s, s1r, s2s, s2r):
    my_r, my_c = lax.axis_index("row"), lax.axis_index("col")
    rows, width = start.shape
    span = 4 * rows
    tiles = (rows + 2 * PAD) // 8
    own_low, own_high = PAD // 8, (PAD + rows) // 8

    def wrap(i, n):
        return lax.rem(i + n, n)

    barrier = pltpu.get_barrier_semaphore()

    def greet(r, c):
        pl.semaphore_signal(barrier, inc=1, device_id=(r, c), device_id_type=MESH)

    near = [(dr, dc) for dr in (-1, 0, 1) for dc in (-1, 0, 1) if (dr, dc) != (0, 0)]
    for dr, dc in near:
        if dr and dc:
            greet(wrap(my_r + dr, nr), wrap(my_c + dc, nc))
    for d in range(1, nc):
        greet(my_r, lax.rem(my_c + d, nc))
    for d in range(1, nr):
        greet(lax.rem(my_r + d, nr), my_c)

    own_el = pltpu.make_async_copy(elev, ev.at[pl.ds(4 * PAD, span), pl.ds(0, 4 * width)], ls.at[0])
    own_el.start()
    own_s = pltpu.make_async_copy(start, sx.at[pl.ds(PAD, rows), pl.ds(0, width)], ls.at[1])
    own_s.start()

    n_i = lax.broadcasted_iota(jnp.int32, (512, 128), 0)
    m_i = lax.broadcasted_iota(jnp.int32, (512, 128), 1)
    for q in range(4):
        perm[:, 128 * q:128 * (q + 1)] = jnp.where(n_i == 4 * m_i + q, 1.0, 0.0).astype(BF16)
    n_t = lax.broadcasted_iota(jnp.int32, (128, 128), 0)
    m_t = lax.broadcasted_iota(jnp.int32, (128, 128), 1)
    for q in range(4):
        hit = ((n_t < 48) & (n_t == 4 * m_t + q)) | ((n_t >= 48) & (n_t == 4 * m_t - 416 + q) & (n_t < 96))
        permt[:, 128 * q:128 * (q + 1)] = jnp.where(hit, 1.0, 0.0).astype(BF16)
    zero = jnp.zeros((8, LANES), F32)
    for j in range(3):
        for q in range(4):
            cols[q, j, 8 * tiles:8 * tiles + 8, :] = zero
        for k in range(16):
            fold[k, j, 0:8, :] = zero
    got_s[16:112, :] = jnp.zeros((96, rows), F32)
    got[96:128, :] = jnp.zeros((32, span), F32)

    def gather(x, matrix, j, r0, rn):
        hi = x.astype(BF16)
        rest = x - hi.astype(F32)
        mid = rest.astype(BF16)
        low = (rest - mid.astype(F32)).astype(BF16)
        m = matrix[...]
        y = jnp.dot(hi, m, preferred_element_type=F32) + jnp.dot(mid, m, preferred_element_type=F32)
        y = y + jnp.dot(low, m, preferred_element_type=F32)
        for k, first_row in enumerate(r0 if isinstance(r0, tuple) else (r0,)):
            for q in range(4):
                tr[4 * j + q, pl.ds(first_row, rn), :] = y[rn * k:rn * (k + 1), 128 * q:128 * (q + 1)]

    def gather_own(b, carry):
        r0 = pl.multiple_of(4 * PAD + 128 * b, 64)
        for j in range(2):
            gather(ev[pl.ds(r0, 128), pl.ds(512 * j, 512)], perm, j, r0, 128)
        return carry

    own_el.wait()
    own_s.wait()
    for b in range(span // 128):
        block = ev[4 * PAD + 128 * b:4 * PAD + 128 * (b + 1), :]
        sent[0:48, 128 * b:128 * (b + 1)] = block[:, 0:128].T[0:48]
        sent[48:96, 128 * b:128 * (b + 1)] = block[:, 4 * width - 128:4 * width].T[80:128]
    sent_s[0:16, :] = sx[PAD:PAD + rows, 0:128].T[0:16]
    sent_s[16:32, :] = sx[PAD:PAD + rows, width - 128:width].T[112:128]
    lane_c = lax.broadcasted_iota(jnp.int32, (24, LANES), 1)
    corners = [(1, 1), (1, -1), (-1, 1), (-1, -1)]
    for k, (dr, dc) in enumerate(corners):
        r0 = 4 * PAD + (span - 48 if dr > 0 else 0)
        q0 = PAD + (rows - 24 if dr > 0 else 0)
        c0, d0 = (4 * width - LANES, width - LANES) if dc > 0 else (0, 0)
        high = ev[r0:r0 + 24, c0:c0 + LANES]
        low = ev[r0 + 24:r0 + 48, c0:c0 + LANES]
        ctl = sx[q0:q0 + 24, d0:d0 + LANES]
        if dc > 0:
            high, low, ctl = pltpu.roll(high, 48, 1), pltpu.roll(low, 96, 1), pltpu.roll(ctl, 112, 1)
        else:
            low, ctl = pltpu.roll(low, 48, 1), pltpu.roll(ctl, 96, 1)
        sent_c[k] = jnp.where(lane_c < 48, high, jnp.where(lane_c < 96, low, ctl))

    lane = lax.broadcasted_iota(jnp.int32, (8, LANES), 1)
    sub = lax.broadcasted_iota(jnp.int32, (8, LANES), 0)
    has_left = jnp.where(my_c > 0, 1, 0)
    has_right = jnp.where(my_c < nc - 1, 1, 0)
    beside = jnp.where(lane < 64, has_right, has_left) > 0
    beside_f = jnp.where(beside, 1.0, 0.0)
    cell_side = ((lane < 9) & (has_right > 0)) | ((lane >= 116) & (has_left > 0))

    def inside_rows(t):
        g = rows * my_r + 8 * t - PAD + sub
        return (g >= 0) & (g < nr * rows)

    def left_shift(u, c):
        r = [pltpu.roll(x, LANES - c, 1) for x in u]
        return [jnp.where(lane < LANES - c, r[j], r[(j + 1) % 3]) for j in range(3)]

    def right_shift(u, c):
        r = [pltpu.roll(x, c, 1) for x in u]
        return [jnp.where(lane < c, r[(j - 1) % 3], r[j]) for j in range(3)]

    def at(t, off=0):
        return pl.ds(pl.multiple_of(8 * t, 8) + off, 8)

    def spread(v):
        x = [v] + [left_shift(v, c) for c in range(1, 4)]
        return [expand4([x[c][j] for c in range(4)]) for j in range(3)]

    def keep_spread(u, t, js=(0, 1, 2)):
        for j in js:
            for q in range(4):
                cols[q, j, at(t), :] = u[j][q]

    def first_near(ts):
        done = []
        for t in ts:
            v = [jnp.where(inside_rows(t), sx[at(t), 128 * j:128 * (j + 1)], 0.0) for j in range(2)]
            done.append((t, spread(v + [v[1]])))
        for t, u in done:
            keep_spread(u, t, (0,))

    def first(ts, js=(0, 1, 2)):
        done = []
        for t in ts:
            keep = inside_rows(t)
            parts = [sx[at(t), 0:128], sx[at(t), 128:256], side[at(t), :]]
            ok = [keep, keep, keep & beside]
            v = [jnp.where(ok[j], parts[j], 0.0) for j in range(3)]
            done.append((t, v, spread(v)))
        for t, v, u in done:
            for j in range(3):
                s_v[j, at(t), :] = v[j]
            keep_spread(u, t, js)

    def rows_first(ts, js=(0, 1, 2)):
        for t in ts:
            i = 8 * t + sub
            okr = inside_rows(t) & (i >= PAD - 12) & (i < PAD + rows + 9)
            for j in js:
                ok = okr & cell_side if j == 2 else okr
                for q in range(4):
                    z = expand4([cols[q, j, at(t, a), :] for a in range(4)])
                    y = []
                    for p in range(4):
                        el = tr[4 * j + q, pl.ds(pl.multiple_of(32 * t, 32) + p, 8, stride=4), :]
                        misfit = el - 0.25 * z[p]
                        w = huber_delta / jnp.maximum(jnp.abs(misfit), huber_delta)
                        wts[4 * p + q, j, at(t), :] = jnp.where(ok, w * 0.0625, 0.0)
                        y.append(jnp.where(ok, w * misfit * 0.25, 0.0))
                    f = reduce4(y)
                    for a in range(4):
                        fold[4 * a + q, j, at(t, 8), :] = f[a]

    def rows_next(ts):
        for t in ts:
            for j in range(3):
                for q in range(4):
                    z = expand4([cols[q, j, at(t, a), :] for a in range(4)])
                    f = reduce4([z[p] * wts[4 * p + q, j, at(t), :] for p in range(4)])
                    for a in range(4):
                        fold[4 * a + q, j, at(t, 8), :] = f[a]

    def collect(t):
        g = []
        for j in range(3):
            h = []
            for q in range(4):
                parts = [fold[4 * a + q, j, at(t, 8 - a), :] for a in range(4)]
                h.append((parts[0] + parts[1]) + (parts[2] + parts[3]))
            g.append(reduce4(h))
        out = [g[j][0] for j in range(3)]
        for c in range(1, 4):
            moved = right_shift([g[j][c] for j in range(3)], c)
            out = [out[j] + moved[j] for j in range(3)]
        rowm = jnp.where(inside_rows(t), 1.0, 0.0)
        return [out[0] * rowm, out[1] * rowm, out[2] * (rowm * beside_f)]

    def finish(src, dst, scale, on):
        def body(ts):
            done = []
            for t in ts:
                out = collect(t)
                new = [out[j] + scale * src[j, at(t), :] for j in range(3)]
                done.append((t, new, spread(new) if on else None))
            for t, new, u in done:
                for j in range(3):
                    dst[j, at(t), :] = new[j]
                if on:
                    keep_spread(u, t)
        return body

    pl.semaphore_wait(barrier, (nr - 1) + (nc - 1) + 4)

    sends = []

    def send_to(dr, dc, src, dst):
        k = len(sends)
        sends.append(pltpu.make_async_remote_copy(
            src_ref=src, dst_ref=dst, send_sem=hs.at[k], recv_sem=hr.at[k],
            device_id=(wrap(my_r + dr, nr), wrap(my_c + dc, nc)), device_id_type=MESH))
        sends[-1].start()

    for dc in (-1, 1):
        part, part_s, to_s = ((pl.ds(0, 48), pl.ds(0, 16), pl.ds(0, 16)) if dc < 0
                              else (pl.ds(48, 48), pl.ds(16, 16), pl.ds(112, 16)))
        send_to(0, dc, sent.at[part], got.at[part])
        send_to(0, dc, sent_s.at[part_s], got_s.at[to_s])
    beside_count = len(sends)
    for k, (dr, dc) in enumerate(corners):
        send_to(dr, dc, sent_c.at[k], got_c.at[k])
    up, down = 48, 40
    send_to(1, 0, start.at[pl.ds(rows - PAD, PAD)], sx.at[pl.ds(0, PAD)])
    send_to(-1, 0, start.at[pl.ds(0, PAD)], sx.at[pl.ds(PAD + rows, PAD)])
    blocks = span // 128
    lax.fori_loop(0, 2, lambda k, c: gather_own(k * (blocks - 1), c), 0)
    send_to(1, 0, tr.at[pl.ds(0, 8), pl.ds(4 * PAD + span - up, up)], tr.at[pl.ds(0, 8), pl.ds(4 * PAD - up, up)])
    send_to(-1, 0, tr.at[pl.ds(0, 8), pl.ds(4 * PAD, down)], tr.at[pl.ds(0, 8), pl.ds(4 * PAD + span, down)])

    lax.fori_loop(1, blocks - 1, gather_own, 0)
    loop(2, 18, 4, first_near)
    loop(2, 17, 3, lambda ts: rows_first(ts, (0,)))
    for copy in sends[:beside_count]:
        copy.wait_recv()
    for b in range(span // 128):
        gather(got[:, 128 * b:128 * (b + 1)].T, permt, 2, 4 * PAD + 128 * b, 128)
    side[PAD:PAD + rows, :] = got_s[...].T

    loop(2, 18, 4, lambda ts: first(ts, (1, 2)))
    loop(2, 17, 3, lambda ts: rows_first(ts, (1, 2)))
    loop(3, 17, 4, finish(s_v, v0, -ridge, True))
    loop(3, 16, 2, rows_next)
    loop(4, 16, 4, finish(v0, v1, ridge - SHIFT, True))
    loop(4, 15, 2, rows_next)
    loop(5, 15, 5, finish(v1, v2, ridge - SHIFT, True))

    def moments(t, accs):
        for j in range(2):
            a, b, c = v0[j, at(t), :], v1[j, at(t), :], v2[j, at(t), :]
            energy = None
            for q in range(4):
                z = expand4([cols[q, j, at(t, k), :] for k in range(4)])
                for p in range(4):
                    e = z[p] * z[p] * wts[4 * p + q, j, at(t), :]
                    energy = e if energy is None else energy + e
            accs = tuple(x + y for x, y in zip(accs, (a * a, a * b, b * b, b * c, c * c, energy)))
        return accs

    accs = lax.fori_loop(5, 14, moments, (zero,) * 6)

    for copy in sends[beside_count:]:
        copy.wait_recv()
    lane2 = lax.broadcasted_iota(jnp.int32, (PAD, LANES), 1)
    lane_d = lax.broadcasted_iota(jnp.int32, (48, LANES), 1)
    turned = []
    for k, (q0, cut) in enumerate(((0, 8), (PAD + rows, 0))):
        from_left, from_right = got_c[2 * k], got_c[2 * k + 1]
        left2 = jnp.concatenate([pltpu.roll(from_left, 48, 1), from_left], 0)
        right2 = jnp.concatenate([from_right, pltpu.roll(from_right, 80, 1)], 0)
        turned.append(jnp.where(lane_d < 48, right2, left2))
        side[q0:q0 + PAD, :] = jnp.where(
            lane2 < 64, pltpu.roll(from_right[cut:cut + PAD], 32, 1), pltpu.roll(from_left[cut:cut + PAD], 16, 1))
    gather(jnp.concatenate(turned, 0), permt, 2, (4 * PAD - 48, 4 * PAD + span), 48)
    edges((0, 2), (18, 20), 4, first)
    edges((0, 2), (17, 20), 1, rows_first)
    edges((0, 3), (17, 20), 6, finish(s_v, v0, -ridge, True))
    edges((0, 3), (16, 19), 2, rows_next)
    edges((1, 4), (16, 19), 6, finish(v0, v1, ridge - SHIFT, True))
    edges((1, 4), (15, 19), 1, rows_next)
    edges((1, 5), (15, 19), 8, finish(v1, v2, ridge - SHIFT, True))
    accs = lax.fori_loop(0, 7, lambda k, a: moments(jnp.where(k < 3, 2 + k, 11 + k), a), accs)

    for k, acc in enumerate(accs):
        one[my_c, k:k + 1, :] = jnp.sum(acc, axis=0, keepdims=True)
    one[my_c, 6:8, :] = jnp.zeros((2, LANES), F32)

    def exchange(buf, send_sem, recv_sem, me, count, target):
        copies = []
        for d in range(1, count):
            copies.append(pltpu.make_async_remote_copy(
                src_ref=buf.at[me], dst_ref=buf.at[me], send_sem=send_sem.at[d], recv_sem=recv_sem.at[me],
                device_id=target(lax.rem(me + d, count)), device_id_type=MESH))
            copies[-1].start()
        return copies

    def arrive(buf, send_sem, recv_sem, me, count, target):
        for d in range(1, count):
            src = lax.rem(me + d, count)
            pltpu.make_async_remote_copy(
                src_ref=buf.at[src], dst_ref=buf.at[src], send_sem=send_sem.at[d], recv_sem=recv_sem.at[src],
                device_id=target(src), device_id_type=MESH).wait_recv()
        parts = [buf[k] for k in range(count)]
        while len(parts) > 1:
            parts = [parts[k] + parts[k + 1] for k in range(0, len(parts), 2)]
        return parts[0]

    sends += exchange(one, s1s, s1r, my_c, nc, lambda s: (my_r, s))
    loop(1, 18, 1, rows_next)
    two[my_r] = arrive(one, s1s, s1r, my_c, nc, lambda s: (my_r, s))
    sends += exchange(two, s2s, s2r, my_r, nr, lambda s: (s, my_c))
    loop(2, 18, 4, finish(v2, v3, ridge - SHIFT, False))
    for copy in sends[:-(nr - 1)]:
        copy.wait_send()
    total = arrive(two, s2s, s2r, my_r, nr, lambda s: (s, my_c))
    total = jnp.broadcast_to(jnp.sum(total, axis=1, keepdims=True), (8, LANES))
    nu = [total[k:k + 1, :] for k in range(6)]
    pairs = [(m, jnp.abs(m)) for m in nu]
    pairs[5] = (nu[5] + (ridge - SHIFT) * nu[4], nu[5] + SHIFT * nu[4])
    step, last, fine = cg_scalars(pairs)

    step, last = ([jnp.broadcast_to(k, (8, LANES)) for k in ks] for ks in (step, last))
    flag[0, 0] = jnp.max(fine)
    use = jnp.broadcast_to(fine, (8, LANES)) > 0.5

    def final(ts):
        for t in ts:
            out_rows = pl.ds(pl.multiple_of(8 * t, 8) - PAD, 8)
            for j in range(2):
                v = [ref[j, at(t), :] for ref in (v0, v1, v2, v3)]
                xa = (step[0] * v[0] + step[1] * v[1]) + step[2] * v[2]
                xa_out[out_rows, 128 * j:128 * (j + 1)] = jnp.where(use, xa, 0.0)
                xb_out[out_rows, 128 * j:128 * (j + 1)] = s_v[j, at(t), :]
                ra_out[out_rows, 128 * j:128 * (j + 1)] = jnp.where(use, last[0] * v[0] + last[1] * v[1], 0.0)
                rb_out[out_rows, 128 * j:128 * (j + 1)] = last[2] * v[2] + last[3] * v[3]

    loop(own_low, own_high, 4, final)
    for copy in sends[-(nr - 1):]:
        copy.wait_send()


def from_behind(block, axis, distance):
    devices = range(lax.axis_size(axis))
    route = [(i - distance, i) for i in devices if i - distance in devices]
    return lax.ppermute(block, axis, route)


def expand_rows(field, table):
    count = field.shape[0] - 3
    outputs = []
    for phase in range(4):
        total = table[phase][0] * field[0:count]
        for offset in range(1, 4):
            total = total + table[phase][offset] * field[offset : offset + count]
        outputs.append(total)
    return jnp.stack(outputs, axis=1).reshape(4 * count, field.shape[1])


def expand_cols(field, table):
    count = field.shape[1] - 3
    outputs = []
    for phase in range(4):
        total = table[phase][0] * field[:, 0:count]
        for offset in range(1, 4):
            total = total + table[phase][offset] * field[:, offset : offset + count]
        outputs.append(total)
    return jnp.stack(outputs, axis=2).reshape(field.shape[0], 4 * count)


def reduce_rows(field, table):
    count = field.shape[0] // 4
    grouped = field.reshape(count, 4, field.shape[1])
    total = None
    for offset in range(4):
        part = table[0][offset] * grouped[:, 0]
        for phase in range(1, 4):
            part = part + table[phase][offset] * grouped[:, phase]
        placed = jnp.pad(part, ((offset, 3 - offset), (0, 0)))
        total = placed if total is None else total + placed
    return total


def reduce_cols(field, table):
    count = field.shape[1] // 4
    grouped = field.reshape(field.shape[0], count, 4)
    total = None
    for offset in range(4):
        part = table[0][offset] * grouped[:, :, 0]
        for phase in range(1, 4):
            part = part + table[phase][offset] * grouped[:, :, phase]
        placed = jnp.pad(part, ((0, 0), (offset, 3 - offset)))
        total = placed if total is None else total + placed
    return total


def extend(tile):
    below = from_behind(tile[:3], "row", -1)
    taller = jnp.concatenate([tile, below], 0)
    beside = from_behind(taller[:, :3], "col", -1)
    return jnp.concatenate([taller, beside], 1)


def fold(partial_value):
    tile_rows = partial_value.shape[0] - 3
    tile_cols = partial_value.shape[1] - 3
    beside = from_behind(partial_value[:, tile_cols:], "col", 1)
    narrow = jnp.concatenate([partial_value[:, :3] + beside, partial_value[:, 3:tile_cols]], 1)
    below = from_behind(narrow[tile_rows:], "row", 1)
    return jnp.concatenate([narrow[:3] + below, narrow[3:tile_rows]], 0)


def squares(residual):
    return lax.psum(jnp.sum(residual * residual), ("row", "col"))


def step_by_step(elevation, start_controls):
    table = TABLE

    def evaluate(tile):
        return expand_cols(expand_rows(extend(tile), table), table)

    def transposed(field):
        return fold(reduce_rows(reduce_cols(field, table), table))

    misfit = elevation - evaluate(start_controls)
    weights = huber_delta / jnp.maximum(jnp.abs(misfit), huber_delta)
    first_term = transposed(weights * misfit)
    controls = start_controls
    residual = first_term - ridge * start_controls
    direction = residual
    norm_now = squares(residual)
    for step in range(ITERS):
        image = transposed(weights * evaluate(direction)) + ridge * direction
        alpha = norm_now / lax.psum(jnp.sum(direction * image), ("row", "col"))
        controls = controls + alpha * direction
        residual = residual - alpha * image
        norm_next = squares(residual)
        direction = residual + norm_next / norm_now * direction
        norm_now = norm_next
    return (controls, residual)


def add_pairs(xa, xb, ra, rb, x, r):
    x[...] = xa[...] + xb[...]
    r[...] = ra[...] + rb[...]


def solution(mesh):
    nr, nc = mesh.shape["row"], mesh.shape["col"]

    def shards(elevation, start_controls):
        rows, width = start_controls.shape
        out = jax.ShapeDtypeStruct((rows, width), F32)
        tall = rows + 2 * PAD
        field = pltpu.VMEM((3, tall, LANES), F32)
        xa, xb, ra, rb, fine = pl.pallas_call(
            functools.partial(kernel, nr, nc),
            out_shape=(out, out, out, out, jax.ShapeDtypeStruct((1, 1), F32)),
            in_specs=[pl.BlockSpec(memory_space=pltpu.HBM)] * 2,
            out_specs=(pl.BlockSpec(memory_space=pltpu.VMEM),) * 4 + (pl.BlockSpec(memory_space=pltpu.SMEM),),
            scratch_shapes=[
                pltpu.VMEM((4 * tall, 4 * width), F32),
                pltpu.VMEM((12, 4 * tall, LANES), F32),
                pltpu.VMEM((tall, width), F32),
                pltpu.VMEM((tall, LANES), F32),
                pltpu.VMEM((4, 24, LANES), F32),
                pltpu.VMEM((4, 24, LANES), F32),
                pltpu.VMEM((96, 4 * rows), F32),
                pltpu.VMEM((128, 4 * rows), F32),
                pltpu.VMEM((32, rows), F32),
                pltpu.VMEM((LANES, rows), F32),
                pltpu.VMEM((4, 3, tall + 8, LANES), F32),
                pltpu.VMEM((16, 3, tall + 8, LANES), F32),
                pltpu.VMEM((16, 3, tall, LANES), F32),
                field, field, field, field, field,
                pltpu.VMEM((512, 512), BF16),
                pltpu.VMEM((128, 512), BF16),
                pltpu.VMEM((nc, 8, LANES), F32),
                pltpu.VMEM((nr, 8, LANES), F32),
                pltpu.SemaphoreType.DMA((16,)),
                pltpu.SemaphoreType.DMA((16,)),
                pltpu.SemaphoreType.DMA((2,)),
                pltpu.SemaphoreType.DMA((nc,)),
                pltpu.SemaphoreType.DMA((nc,)),
                pltpu.SemaphoreType.DMA((nr,)),
                pltpu.SemaphoreType.DMA((nr,)),
            ],
            compiler_params=pltpu.CompilerParams(
                collective_id=0, has_side_effects=True, vmem_limit_bytes=60 * 1024 * 1024
            ),
        )(elevation, start_controls)
        x, r = lax.cond(fine[0, 0] > 0.5, lambda: (xb, rb), lambda: step_by_step(elevation, start_controls))
        return pl.pallas_call(add_pairs, out_shape=(out, out))(xa, x, ra, r)

    return jax.shard_map(
        shards,
        mesh=mesh,
        in_specs=(P("row", "col"), P("row", "col")),
        out_specs=(P("row", "col"), P("row", "col")),
        check_vma=False,
    )
```
